1024 devices in a mesh: we: 8 (over x_lo, y), sn: 128 (over x_hi, z, core).
Axes of the slice: x: 4 (x_hi: 2, x_lo: 2; x = x_hi * 2 + x_lo), y: 4, z: 32, core: 2. Of those that a mesh axis runs over, the one named last changes fastest.
Arguments:
- velocity: float32 [3, 32, 1536, 128], P(None, 'we', 'sn'), may hold values from -6 to 6
- stress: float32 [6, 32, 1536, 128], P(None, 'we', 'sn'), may hold values from -6 to 6
- memory: float32 [6, 32, 1536, 128], P(None, 'we', 'sn'), may hold values from -3 to 3
- material_code: int32 [32, 1536, 128], P('we', 'sn'), may hold values from 0 to 15
- block_scale: float32 [8, 384, 4], P('we', 'sn'), may hold values from 0.5 to 2
- material_table: float32 [6, 16], replicated, may hold values from 0.2 to 3, as said below
- source_cell: int32 [8, 128, 4], P('we', 'sn'), may hold values from 0 to 6143, as said below
- source_amp: float32 [8, 128, 4, 4], P('we', 'sn'), may hold values from -24 to 24
Outputs:
- velocity_out: float32 [3, 32, 1536, 128], P(None, 'we', 'sn')
- stress_out: float32 [6, 32, 1536, 128], P(None, 'we', 'sn')
- memory_out: float32 [6, 32, 1536, 128], P(None, 'we', 'sn')
The draws below stay inside these ranges and needn't reach their ends.
Inputs may be any that keep to these rules, and one draw needn't show every extreme that they name: Rows of material_table lie in: buoyancy 0.6 to 1.4, first Lame parameter 0.5 to 2, shear modulus 0.3 to 1.5, decay 0.5 to 0.98, weight 0.2 to 0.8, cohesion 0.3 to 3. `source_cell`: each entry is c = x 12 * 128 + y * 128 + z for a cell (x, y, z) of the device's own block; cells may repeat.
All inputs are finite; a program needn't handle non-finite values.
Results may differ from the reference program's by a relative error of at most 0.0001.
Values sent between devices are 32-bit elements; how exact they have to be, the bound alone decides.
A program may use at most 32 MiB of HBM per device.

```python
import math
import jax
import jax.numpy as jnp
from jax import lax

CX = 4
CY = 12
CZ = 128
STEPS = 4
NMAT = 16
BLK = 4
BLKZ = 32
NSRC_DEV = 4
DEV_WE = 8
DEV_SN = 128
NX = 32
NY = 1536
NZ = 128


def draw_material_table(key, part):
    uniform_draw = jax.random.uniform(key, (6, NMAT), jnp.float32)
    lower = jnp.array([0.6, 0.5, 0.3, 0.5, 0.2, 0.3], jnp.float32)
    upper = jnp.array([1.4, 2.0, 1.5, 0.98, 0.8, 3.0], jnp.float32)
    return lower[:, None] + (upper - lower)[:, None] * uniform_draw


def draw_source_cell(key, part):
    picks = jax.random.randint(jax.random.fold_in(key, 17), (DEV_WE, DEV_SN, NSRC_DEV), 0, CX * CY * CZ, jnp.int32)
    picks = picks.at[0, 0, 0].set(0)
    return picks.at[DEV_WE - 1, DEV_SN - 1, NSRC_DEV - 1].set(CX * CY * CZ - 1)


def place_ends(entries, rng, smallest, top_value):
    spot = [jax.random.randint(jax.random.fold_in(rng, axis), (), 0, length) for axis, length in enumerate(entries.shape)]
    main_axis = entries.shape.index(max(entries.shape))
    beside = spot[:main_axis] + [(spot[main_axis] + 1) % entries.shape[main_axis]] + spot[main_axis + 1:]
    return entries.at[tuple(spot)].set(smallest).at[tuple(beside)].set(top_value)


def shard_levels(key, extent, split, smallest, top_value):
    def one(dim, parts):
        steps = jax.random.uniform(jax.random.fold_in(jax.random.fold_in(key, 6), dim), (parts,), jnp.float32, smallest / len(split), top_value / len(split))
        return jnp.repeat(jnp.exp(steps), extent[dim] // parts).reshape((-1,) + (1,) * (len(extent) - dim - 1))

    factor_of = one(*split[0])
    for cut in split[1:]:
        factor_of = factor_of * one(*cut)
    return factor_of


def noise(rng, dims, width, bound, shards=(), dtype=jnp.bfloat16):
    entries = jax.random.normal(rng, dims, jnp.float32) * width
    if len(shards) > 0:
        entries = shard_levels(rng, dims, shards, -0.22, 0.18) * entries
    return jnp.clip(entries, min=-bound, max=bound).astype(dtype)


def setup_inputs(seed: int = 0) -> dict:
    arg_keys = jax.random.split(jax.random.key(seed), 9)
    velocity = noise(arg_keys[0], (3, NX, NY, NZ), 1.0, 6.0, ((1, 8), (2, 128)), jnp.float32)
    stress = noise(arg_keys[1], (6, NX, NY, NZ), 1.0, 6.0, ((1, 8), (2, 128)), jnp.float32)
    memory = noise(arg_keys[2], (6, NX, NY, NZ), 0.5, 3.0, ((1, 8), (2, 128)), jnp.float32)
    material_code = place_ends(jax.random.randint(arg_keys[3], (NX, NY, NZ), 0, NMAT), jax.random.fold_in(arg_keys[3], 1), 0, NMAT - 1).astype(jnp.int32)
    block_scale = jnp.clip(jnp.exp(math.log(2.0) - 1.3862944 * jax.random.uniform(arg_keys[4], (NX // BLK, NY // BLK, NZ // BLKZ), jnp.float32) ** shard_levels(arg_keys[4], (NX // BLK, NY // BLK, NZ // BLKZ), ((0, 8), (1, 128)), -0.2, 0.2)), 0.5, 2.0)
    material_table = draw_material_table(jax.random.fold_in(arg_keys[8], 71), 0)
    source_cell = draw_source_cell(jax.random.fold_in(arg_keys[8], 71), 0)
    source_amp = noise(arg_keys[7], (DEV_WE, DEV_SN, NSRC_DEV, STEPS), 4.0, 24.0, ((0, 8), (1, 128)), jnp.float32)
    return {"velocity": velocity, "stress": stress, "memory": memory, "material_code": material_code, "block_scale": block_scale, "material_table": material_table, "source_cell": source_cell, "source_amp": source_amp}


inner_coef = 9.0 / 8.0
outer_coef = 1.0 / 24.0
time_step = 0.08
friction = 0.4

def shifted(padded, along_dim, offset):
    length = padded.shape[along_dim] - 4
    return lax.slice_in_dim(padded, 2 + offset, 2 + offset + length, axis=along_dim)

def forward(padded, along_dim):
    return inner_coef * (shifted(padded, along_dim, 1) - shifted(padded, along_dim, 0)) - outer_coef * (shifted(padded, along_dim, 2) - shifted(padded, along_dim, -1))

def backward(padded, along_dim):
    return inner_coef * (shifted(padded, along_dim, 0) - shifted(padded, along_dim, -1)) - outer_coef * (shifted(padded, along_dim, 1) - shifted(padded, along_dim, -2))

def depth_pad(fields):
    return jnp.pad(fields, ((0, 0), (0, 0), (0, 0), (2, 2)))

def velocity_step(velocity, stress, east_pad, north_pad, buoyancy):
    depth_stress = depth_pad(stress[1::2])
    force_east = forward(east_pad[0], 0) + backward(north_pad[0], 1) + backward(depth_stress[0], 2)
    force_north = backward(east_pad[2], 0) + forward(north_pad[2], 1) + backward(depth_stress[1], 2)
    force_depth = backward(east_pad[1], 0) + backward(north_pad[1], 1) + forward(depth_stress[2], 2)
    return velocity + time_step * buoyancy * jnp.stack([force_east, force_north, force_depth])

def stress_step(stress, memory, east_vel, north_vel, velocity, lame, shear_mod, decay, weight):
    depth_vel = depth_pad(velocity)
    rate_ee = backward(east_vel[0], 0)
    north_east = forward(east_vel[1], 0)
    depth_east = forward(east_vel[2], 0)
    east_north = forward(north_vel[0], 1)
    rate_nn = backward(north_vel[1], 1)
    depth_north = forward(north_vel[2], 1)
    east_depth = forward(depth_vel[0], 2)
    north_depth = forward(depth_vel[1], 2)
    rate_dd = backward(depth_vel[2], 2)
    volume_rate = rate_ee + rate_nn + rate_dd
    rates = jnp.stack([lame * volume_rate + 2.0 * shear_mod * rate_ee, shear_mod * (east_depth + depth_east), shear_mod * (east_north + north_east), shear_mod * (north_depth + depth_north), lame * volume_rate + 2.0 * shear_mod * rate_nn, lame * volume_rate + 2.0 * shear_mod * rate_dd])
    memory_new = decay * memory + (1.0 - decay) * weight * rates
    trial = stress + time_step * (rates - 0.5 * (memory + memory_new))
    return (trial, memory_new)

def plastic(trial, cohesion):
    normal_mask = jnp.array([1.0, 0.0, 0.0, 0.0, 1.0, 1.0], jnp.float32)[:, None, None, None]
    square_weights = jnp.array([0.5, 1.0, 1.0, 1.0, 0.5, 0.5], jnp.float32)[:, None, None, None]
    mean_stress = (trial[0] + trial[4] + trial[5]) / 3.0
    deviator = trial - normal_mask * mean_stress
    second_inv = lax.optimization_barrier(jnp.sum(square_weights * deviator * deviator, 0))
    yield_level = cohesion + friction * jax.nn.softplus(-mean_stress)
    scaled = second_inv / (yield_level * yield_level)
    factor = lax.rsqrt(jnp.sqrt(1.0 + scaled * scaled))
    return normal_mask * mean_stress + factor * deviator

def reference(velocity, stress, memory, material_code, block_scale, material_table, source_cell, source_amp):
    table_rows = material_table[:, material_code]
    scale_full = jnp.repeat(jnp.repeat(jnp.repeat(block_scale, BLK, 0), BLK, 1), BLKZ, 2)
    buoyancy = table_rows[0]
    lame = table_rows[1] * scale_full
    shear_mod = table_rows[2] * scale_full
    decay = table_rows[3]
    weight = table_rows[4]
    cohesion = table_rows[5]
    shape = source_cell.shape
    device_east = lax.broadcasted_iota(jnp.int32, shape, 0)
    device_north = lax.broadcasted_iota(jnp.int32, shape, 1)
    east_cell = device_east * CX + source_cell // (CY * CZ)
    north_cell = device_north * CY + source_cell // CZ % CY
    depth_cell = source_cell % CZ
    source_cells = ((east_cell * NY + north_cell) * NZ + depth_cell).reshape(-1).astype(jnp.int32)
    strengths = source_amp.reshape(-1, STEPS)
    normal_rows = jnp.array([0, 4, 5], jnp.int32)
    for turn_index in range(STEPS):
        east_pad = jnp.pad(stress[0:3], ((0, 0), (2, 2), (0, 0), (0, 0)))
        north_pad = jnp.pad(stress[2:5], ((0, 0), (0, 0), (2, 2), (0, 0)))
        velocity = velocity_step(velocity, stress, east_pad, north_pad, buoyancy)
        east_vel = jnp.pad(velocity, ((0, 0), (2, 2), (0, 0), (0, 0)))
        north_vel = jnp.pad(velocity, ((0, 0), (0, 0), (2, 2), (0, 0)))
        trial, memory = stress_step(stress, memory, east_vel, north_vel, velocity, lame, shear_mod, decay, weight)
        flat = trial.reshape(6, -1)
        flat = flat.at[normal_rows[:, None], source_cells[None, :]].add(time_step * strengths[:, turn_index][None, :])
        trial = flat.reshape(stress.shape)
        stress = plastic(trial, cohesion)
    return (velocity, stress, memory)
```

```python
import functools

import jax
import jax.numpy as jnp
from jax import lax
from jax.experimental import pallas as pl
from jax.experimental.pallas import tpu as pltpu
from jax.sharding import PartitionSpec as P

STEPS = 4
BLK = 4
BLKZ = 32
MESH = pl.DeviceIdType.MESH

inner_coef = 9.0 / 8.0
outer_coef = 1.0 / 24.0
time_step = 0.08
friction = 0.4
log2_e = 1.4426950408889634
ln_2 = 0.6931471805599453

LAYERS = 8
ROWS = 16

TO_HIGH = ((4, 0), (5, 1), (5, 1))
TO_LOW = ((0, 4), (1, 5), (1, 5))


def forward(layers, i):
    return combine(layers, (i + 1, i, i + 2, i - 1))


def backward(layers, i):
    return combine(layers, (i, i - 1, i + 1, i - 2))


def combine(layers, at):
    terms = []
    for index, coef in zip(at, (inner_coef, -inner_coef, -outer_coef, outer_coef)):
        if 0 <= index < len(layers):
            terms.append((coef, layers[index]))
    total = None
    for coef, layer in terms:
        total = coef * layer if total is None else total + coef * layer
    return total


def moved(field, offset, axis):
    size = field.shape[axis]
    return pltpu.roll(field, (-offset) % size, axis)


def forward_rows(field):
    return inner_coef * (moved(field, 1, 1) - field) - outer_coef * (
        moved(field, 2, 1) - moved(field, -1, 1)
    )


def backward_rows(field):
    return inner_coef * (field - moved(field, -1, 1)) - outer_coef * (
        moved(field, 1, 1) - moved(field, -2, 1)
    )


def kernel(
    counts,
    vel_in,
    str_in,
    mem_in,
    code_in,
    scale,
    table,
    cells,
    amps,
    vel_out,
    str_out,
    mem_out,
    V,
    S,
    M,
    CODE,
    G,
    RA,
    RB,
    DB,
    PROP,
    SRC,
    load_sem,
    first_send,
    first_recv,
    send_sem,
    recv_sem,
):
    n_we, n_sn = counts
    we = lax.axis_index("we")
    sn = lax.axis_index("sn")
    east, west = lax.rem(we + 1, n_we), lax.rem(we + n_we - 1, n_we)
    north, south = lax.rem(sn + 1, n_sn), lax.rem(sn + n_sn - 1, n_sn)
    side = {1: east, -1: west}
    along = {1: north, -1: south}
    off_x = {1: jnp.where(we == n_we - 1, 2, 0), -1: jnp.where(we == 0, 2, 0)}
    off_y = {1: jnp.where(sn == n_sn - 1, 2, 0), -1: jnp.where(sn == 0, 2, 0)}

    def to(dx, dy):
        return (
            side[dx] if dx else we,
            along[dy] if dy else sn,
        )

    around = [(dx, dy) for dx in (-1, 0, 1) for dy in (-1, 0, 1) if dx or dy]

    own_v = V.at[:, 2:6, 2:14, :]
    own_s = S.at[:, :, 2:14, :]
    own_m = M.at[:, :, 2:14, :]
    loads = [
        pltpu.make_async_copy(str_in, own_s, load_sem.at[0]),
        pltpu.make_async_copy(code_in, CODE.at[2:6, 2:14, :], load_sem.at[1]),
        pltpu.make_async_copy(vel_in, own_v, load_sem.at[2]),
        pltpu.make_async_copy(mem_in, own_m, load_sem.at[3]),
    ]
    for load in loads:
        load.start()

    zero_slot = jnp.zeros((2, 3, LAYERS, ROWS, 128), jnp.float32)
    RA[0:2] = zero_slot
    RB[0:2] = zero_slot
    edge_rows = jnp.zeros((6, 4, 2, 128), jnp.float32)
    S[:, :, 0:2, :] = edge_rows
    S[:, :, 14:16, :] = edge_rows
    G[0, 7] = jnp.zeros((ROWS, 128), jnp.float32)
    G[1, 0] = jnp.zeros((ROWS, 128), jnp.float32)
    G[2, 0] = jnp.zeros((ROWS, 128), jnp.float32)

    barrier = pltpu.get_barrier_semaphore()
    for dx, dy in around:
        pl.semaphore_signal(barrier, inc=1, device_id=to(dx, dy), device_id_type=MESH)
    pl.semaphore_wait(barrier, len(around))

    first = []

    def send_first(src, dst, dx, dy):
        k = len(first)
        first.append(
            pltpu.make_async_remote_copy(
                src_ref=src,
                dst_ref=dst,
                send_sem=first_send.at[k],
                recv_sem=first_recv.at[k],
                device_id=to(dx, dy),
                device_id_type=MESH,
            )
        )
        first[-1].start()

    send_first(vel_in.at[:, 2:4], V.at[:, 0:2, 2:14, :], 1, 0)
    send_first(vel_in.at[:, 0:2], V.at[:, 6:8, 2:14, :], -1, 0)
    send_first(vel_in.at[:, :, 10:12, :], V.at[:, 2:6, 0:2, :], 0, 1)
    send_first(vel_in.at[:, :, 0:2, :], V.at[:, 2:6, 14:16, :], 0, -1)
    send_first(code_in.at[2:4], CODE.at[0:2, 2:14, :], 1, 0)
    send_first(code_in.at[0:2], CODE.at[6:8, 2:14, :], -1, 0)
    send_first(code_in.at[:, 10:12, :], CODE.at[2:6, 0:2, :], 0, 1)
    send_first(code_in.at[:, 0:2, :], CODE.at[2:6, 14:16, :], 0, -1)

    loads[0].wait()

    block = (4, ROWS, 128)
    lane = lax.broadcasted_iota(jnp.int32, (1, 1, 128), 2)
    row = lax.broadcasted_iota(jnp.int32, (1, ROWS, 128), 1)

    def lane_coef(coef, offset):
        inside = (lane + offset >= 0) & (lane + offset < 128)
        return jnp.where(inside, coef, 0.0)

    def forward_lanes(field):
        return (
            lane_coef(inner_coef, 1) * moved(field, 1, 2)
            - inner_coef * field
            - lane_coef(outer_coef, 2) * moved(field, 2, 2)
            + lane_coef(outer_coef, -1) * moved(field, -1, 2)
        )

    def backward_lanes(field):
        return (
            inner_coef * field
            - lane_coef(inner_coef, -1) * moved(field, -1, 2)
            - lane_coef(outer_coef, 1) * moved(field, 1, 2)
            + lane_coef(outer_coef, -2) * moved(field, -2, 2)
        )

    def force(component, along_x, field_x, rest):
        layers = [field_x[i] for i in range(4)]
        for i in range(-2, 6):
            part = along_x(layers, i)
            if part is None:
                continue
            if 0 <= i < 4:
                part = part + rest[i]
            G[component, i + 2] = part

    def step(t, carry):
        slot = lax.rem(t, 2)
        copies = []

        def send(src, ref, dst, dx, dy):
            k = len(copies)
            there = slot
            if dx and dy:
                there = slot + jnp.maximum(off_x[dx], off_y[dy])
            elif dx:
                there = slot + off_x[dx]
            else:
                there = slot + off_y[dy]
            copies.append(
                pltpu.make_async_remote_copy(
                    src_ref=src,
                    dst_ref=ref.at[(there,) + dst],
                    send_sem=send_sem.at[slot, k],
                    recv_sem=recv_sem.at[slot, k],
                    device_id=to(dx, dy),
                    device_id_type=MESH,
                )
            )
            copies[-1].start()

        def send_x(c):
            for dx, (here, there) in ((1, TO_HIGH[c]), (-1, TO_LOW[c])):
                send(
                    G.at[c, pl.ds(here, 3), pl.ds(2, 12), :],
                    RA,
                    (c, pl.ds(there, 3), pl.ds(2, 12), slice(None)),
                    dx,
                    0,
                )

        sxx, sxz, sxy, syz, syy, szz = (S[c] for c in range(6))
        force(0, forward, sxx, backward_rows(sxy) + backward_lanes(sxz))
        send_x(0)
        force(1, backward, sxy, forward_rows(syy) + backward_lanes(syz))
        send_x(1)
        force(2, backward, sxz, backward_rows(syz) + forward_lanes(szz))
        send_x(2)

        everything = slice(None)
        for dy, (here, there) in ((1, (12, 0)), (-1, (0, 12))):
            send(
                G.at[:, pl.ds(2, 4), pl.ds(here, 4), :],
                RB,
                (everything, pl.ds(2, 4), pl.ds(there, 4), everything),
                0,
                dy,
            )
        for dx in (1, -1):
            for dy in (1, -1):
                from_l, to_l = (6, 2) if dx == 1 else (0, 4)
                from_r, to_r = (12, 0) if dy == 1 else (2, 14)
                send(
                    G.at[:, pl.ds(from_l, 2), pl.ds(from_r, 2), :],
                    RA,
                    (everything, pl.ds(to_l, 2), pl.ds(to_r, 2), everything),
                    dx,
                    dy,
                )
                from_l, to_l = (4, 0) if dx == 1 else (2, 6)
                from_r, to_r = (14, 2) if dy == 1 else (0, 12)
                send(
                    G.at[:, pl.ds(from_l, 2), pl.ds(from_r, 2), :],
                    RB,
                    (everything, pl.ds(to_l, 2), pl.ds(to_r, 2), everything),
                    dx,
                    dy,
                )

        @pl.when(t == 0)
        def _():
            for load in loads[1:]:
                load.wait()
            for copy in first:
                copy.wait()

            def look_up(code, r):
                values = [table[r, k] for k in range(16)]
                for bit in range(4):
                    chosen = (code & (1 << bit)) != 0
                    values = [
                        jnp.where(chosen, values[2 * k + 1], values[2 * k])
                        for k in range(len(values) // 2)
                    ]
                return values[0]

            layer = lax.broadcasted_iota(jnp.int32, (LAYERS, ROWS, 128), 0)
            rows = lax.broadcasted_iota(jnp.int32, (LAYERS, ROWS, 128), 1)
            inside = (
                (layer >= jnp.where(we == 0, 2, 0))
                & (layer < jnp.where(we == n_we - 1, 6, 8))
                & (rows >= jnp.where(sn == 0, 2, 0))
                & (rows < jnp.where(sn == n_sn - 1, 14, 16))
            )
            DB[...] = jnp.where(inside, time_step * look_up(CODE[...], 0), 0.0)
            for c in range(3):
                V[c] = jnp.where(inside, V[c], 0.0)

            moduli = jnp.zeros((1, ROWS, 128), jnp.float32)
            for j in range(3):
                for k in range(128 // BLKZ):
                    here = (
                        (row >= 2 + BLK * j)
                        & (row < 2 + BLK * (j + 1))
                        & (lane >= BLKZ * k)
                        & (lane < BLKZ * (k + 1))
                    )
                    moduli = jnp.where(here, scale[0, j, k], moduli)
            code = CODE[2:6]
            PROP[0] = look_up(code, 1) * moduli
            PROP[1] = look_up(code, 2) * moduli
            decay = look_up(code, 3)
            gain = (1.0 - decay) * look_up(code, 4)
            PROP[2] = decay
            PROP[3] = gain
            PROP[4] = time_step * (1.0 - 0.5 * gain)
            PROP[5] = (0.5 * time_step) * (1.0 + decay)
            PROP[6] = look_up(code, 5)

            cell = (
                (
                    lax.broadcasted_iota(jnp.int32, block, 0) * 12
                    + lax.broadcasted_iota(jnp.int32, block, 1)
                    - 2
                )
                * 128
                + lax.broadcasted_iota(jnp.int32, block, 2)
            )
            for n in range(STEPS):
                added = jnp.zeros(block, jnp.float32)
                for k in range(4):
                    added = added + jnp.where(
                        cell == cells[0, 0, k], time_step * amps[0, 0, k, n], 0.0
                    )
                SRC[n] = added

        for copy in copies:
            copy.wait()

        for c in range(3):
            V[c] = V[c] + DB[...] * (G[c] + RA[slot, c] + RB[slot, c])

        def forward_x(c):
            return inner_coef * (V[c, 3:7] - V[c, 2:6]) - outer_coef * (V[c, 4:8] - V[c, 1:5])

        def backward_x(c):
            return inner_coef * (V[c, 2:6] - V[c, 1:5]) - outer_coef * (V[c, 3:7] - V[c, 0:4])

        ve, vn, vd = (V[c, 2:6] for c in range(3))
        exx = backward_x(0)
        eyy = backward_rows(vn)
        ezz = backward_lanes(vd)
        exz = forward_lanes(ve) + forward_x(2)
        exy = forward_rows(ve) + forward_x(1)
        eyz = forward_lanes(vn) + forward_rows(vd)
        lame, shear = PROP[0], PROP[1]
        volume = lame * (exx + eyy + ezz)
        twice = shear + shear
        rates = (
            volume + twice * exx,
            shear * exz,
            shear * exy,
            shear * eyz,
            volume + twice * eyy,
            volume + twice * ezz,
        )
        trial = []
        for c in range(6):
            memory = M[c]
            M[c] = PROP[2] * memory + PROP[3] * rates[c]
            trial.append(S[c] + PROP[4] * rates[c] - PROP[5] * memory)
        added = SRC[t]
        for c in (0, 4, 5):
            trial[c] = trial[c] + added
        mean = (trial[0] + trial[4] + trial[5]) * (1.0 / 3.0)
        for c in (0, 4, 5):
            trial[c] = trial[c] - mean
        normal = trial[0] * trial[0] + trial[4] * trial[4] + trial[5] * trial[5]
        second = 0.5 * normal + (
            trial[1] * trial[1] + trial[2] * trial[2] + trial[3] * trial[3]
        )
        soft = jnp.maximum(-mean, 0.0) + ln_2 * jnp.log2(1.0 + jnp.exp2(-log2_e * jnp.abs(mean)))
        level = PROP[6] + friction * soft
        scaled = second / (level * level)
        factor = jnp.exp2(-0.25 * jnp.log2(1.0 + scaled * scaled))
        own = (row >= 2) & (row < 14)
        for c in range(6):
            new = factor * trial[c]
            if c in (0, 4, 5):
                new = mean + new
            S[c] = jnp.where(own, new, 0.0)
        return carry

    lax.fori_loop(0, STEPS, step, 0)

    stores = [
        pltpu.make_async_copy(own_v, vel_out, load_sem.at[0]),
        pltpu.make_async_copy(own_s, str_out, load_sem.at[1]),
        pltpu.make_async_copy(own_m, mem_out, load_sem.at[2]),
    ]
    for store in stores:
        store.start()
    for store in stores:
        store.wait()


def solution(mesh):
    counts = (mesh.shape["we"], mesh.shape["sn"])
    f32 = jnp.float32

    def shards(velocity, stress, memory, code, scale, table, cells, amps):
        hbm = pl.BlockSpec(memory_space=pl.ANY)
        smem = pl.BlockSpec(memory_space=pltpu.SMEM)
        return pl.pallas_call(
            functools.partial(kernel, counts),
            out_shape=tuple(
                jax.ShapeDtypeStruct(a.shape, f32) for a in (velocity, stress, memory)
            ),
            in_specs=[hbm] * 4 + [smem] * 4,
            out_specs=(hbm,) * 3,
            scratch_shapes=[
                pltpu.VMEM((3, LAYERS, ROWS, 128), f32),
                pltpu.VMEM((6, 4, ROWS, 128), f32),
                pltpu.VMEM((6, 4, ROWS, 128), f32),
                pltpu.VMEM((LAYERS, ROWS, 128), jnp.int32),
                pltpu.VMEM((3, LAYERS, ROWS, 128), f32),
                pltpu.VMEM((4, 3, LAYERS, ROWS, 128), f32),
                pltpu.VMEM((4, 3, LAYERS, ROWS, 128), f32),
                pltpu.VMEM((LAYERS, ROWS, 128), f32),
                pltpu.VMEM((7, 4, ROWS, 128), f32),
                pltpu.VMEM((STEPS, 4, ROWS, 128), f32),
                pltpu.SemaphoreType.DMA((4,)),
                pltpu.SemaphoreType.DMA((8,)),
                pltpu.SemaphoreType.DMA((8,)),
                pltpu.SemaphoreType.DMA((2, 16)),
                pltpu.SemaphoreType.DMA((2, 16)),
            ],
            compiler_params=pltpu.CompilerParams(
                collective_id=0, has_side_effects=True, vmem_limit_bytes=16 * 1024 * 1024
            ),
        )(velocity, stress, memory, code, scale, table, cells, amps)

    in_specs = (
        P(None, "we", "sn", None),
        P(None, "we", "sn", None),
        P(None, "we", "sn", None),
        P("we", "sn", None),
        P("we", "sn", None),
        P(),
        P("we", "sn", None),
        P("we", "sn", None, None),
    )
    out_specs = (P(None, "we", "sn", None),) * 3
    return jax.shard_map(shards, mesh=mesh, in_specs=in_specs, out_specs=out_specs, check_vma=False)
```

```python
import functools

import jax
import jax.numpy as jnp
from jax import lax
from jax.experimental import pallas as pl
from jax.experimental.pallas import tpu as pltpu
from jax.sharding import PartitionSpec as P

STEPS = 4
BLK = 4
BLKZ = 32
MESH = pl.DeviceIdType.MESH

inner_coef = 9.0 / 8.0
outer_coef = 1.0 / 24.0
time_step = 0.08
friction = 0.4
log2_e = 1.4426950408889634
ln_2 = 0.6931471805599453

LAYERS = 8
ROWS = 16

TO_HIGH = ((4, 0), (5, 1), (5, 1))
TO_LOW = ((0, 4), (1, 5), (1, 5))


def forward(layers, i):
    return combine(layers, (i + 1, i, i + 2, i - 1))


def backward(layers, i):
    return combine(layers, (i, i - 1, i + 1, i - 2))


def combine(layers, at):
    terms = []
    for index, coef in zip(at, (inner_coef, -inner_coef, -outer_coef, outer_coef)):
        if 0 <= index < len(layers):
            terms.append((coef, layers[index]))
    total = None
    for coef, layer in terms:
        total = coef * layer if total is None else total + coef * layer
    return total


def moved(field, offset, axis):
    size = field.shape[axis]
    return pltpu.roll(field, (-offset) % size, axis)


def forward_rows(field):
    return inner_coef * (moved(field, 1, 1) - field) - outer_coef * (
        moved(field, 2, 1) - moved(field, -1, 1)
    )


def backward_rows(field):
    return inner_coef * (field - moved(field, -1, 1)) - outer_coef * (
        moved(field, 1, 1) - moved(field, -2, 1)
    )


def kernel(
    counts,
    vel_in,
    str_in,
    mem_in,
    code_in,
    scale_in,
    table_in,
    cells_in,
    amps_in,
    vel_out,
    str_out,
    mem_out,
    V,
    S,
    M,
    CODE,
    G,
    RA,
    RB,
    DB,
    PROP,
    SRC,
    scale,
    table,
    cells,
    amps,
    load_sem,
    small_sem,
    first_send,
    first_recv,
    send_sem,
    recv_sem,
):
    n_we, n_sn = counts
    we = lax.axis_index("we")
    sn = lax.axis_index("sn")
    side = {
        0: we,
        1: jnp.minimum(we + 1, n_we - 1),
        -1: jnp.maximum(we - 1, 0),
    }
    along = {
        0: sn,
        1: jnp.minimum(sn + 1, n_sn - 1),
        -1: jnp.maximum(sn - 1, 0),
    }
    has_x = {1: we < n_we - 1, -1: we > 0}
    has_y = {1: sn < n_sn - 1, -1: sn > 0}

    def there(dx, dy):
        if dx and dy:
            return has_x[dx] & has_y[dy]
        return has_x[dx] if dx else has_y[dy]

    around = [(dx, dy) for dx in (1, -1) for dy in (1, -1)]
    around += [(0, 1), (0, -1), (1, 0), (-1, 0)]

    RA[0] = jnp.zeros((3, LAYERS, ROWS, 128), jnp.float32)
    RB[0] = jnp.zeros((3, LAYERS, ROWS, 128), jnp.float32)

    barrier = pltpu.get_barrier_semaphore()
    for dx, dy in around:

        @pl.when(there(dx, dy))
        def _():
            pl.semaphore_signal(
                barrier, inc=1, device_id=(side[dx], along[dy]), device_id_type=MESH
            )

    loads = []
    for n, (src, dst, first) in enumerate(((str_in, S, 0), (code_in, CODE, 2), (vel_in, V, 2), (mem_in, M, 0))):
        for x in range(4):
            if src is code_in:
                pair = src.at[:, x, :], dst.at[first + x, 2:14, :]
            else:
                pair = src.at[:, :, x, :], dst.at[:, first + x, 2:14, :]
            loads.append(pltpu.make_async_copy(*pair, load_sem.at[n, x]))
            loads[-1].start()
    small = [
        pltpu.make_async_copy(src, dst, small_sem.at[n])
        for n, (src, dst) in enumerate(
            ((scale_in, scale), (table_in, table), (cells_in, cells), (amps_in, amps))
        )
    ]
    for load in small:
        load.start()

    edge_rows = jnp.zeros((6, 4, 2, 128), jnp.float32)
    S[:, :, 0:2, :] = edge_rows
    S[:, :, 14:16, :] = edge_rows
    G[0, 7] = jnp.zeros((ROWS, 128), jnp.float32)
    G[1, 0] = jnp.zeros((ROWS, 128), jnp.float32)
    G[2, 0] = jnp.zeros((ROWS, 128), jnp.float32)
    RA[1] = jnp.zeros((3, LAYERS, ROWS, 128), jnp.float32)
    RB[1] = jnp.zeros((3, LAYERS, ROWS, 128), jnp.float32)

    block = (4, ROWS, 128)
    lane = lax.broadcasted_iota(jnp.int32, (1, 1, 128), 2)
    row = lax.broadcasted_iota(jnp.int32, (1, ROWS, 128), 1)

    def lane_coef(coef, offset):
        inside = (lane + offset >= 0) & (lane + offset < 128)
        return jnp.where(inside, coef, 0.0)

    def forward_lanes(field):
        return (
            lane_coef(inner_coef, 1) * moved(field, 1, 2)
            - inner_coef * field
            - lane_coef(outer_coef, 2) * moved(field, 2, 2)
            + lane_coef(outer_coef, -1) * moved(field, -1, 2)
        )

    def backward_lanes(field):
        return (
            inner_coef * field
            - lane_coef(inner_coef, -1) * moved(field, -1, 2)
            - lane_coef(outer_coef, 1) * moved(field, 1, 2)
            + lane_coef(outer_coef, -2) * moved(field, -2, 2)
        )

    def force(component, along_x, field_x, rest):
        layers = [field_x[i] for i in range(4)]
        for i in range(-2, 6):
            part = along_x(layers, i)
            if part is None:
                continue
            if 0 <= i < 4:
                part = part + rest[i]
            G[component, i + 2] = part

    def forces():
        sxx, sxz, sxy, syz, syy, szz = (S[c] for c in range(6))
        force(0, forward, sxx, backward_rows(sxy) + backward_lanes(sxz))
        force(1, backward, sxy, forward_rows(syy) + backward_lanes(syz))
        force(2, backward, sxz, backward_rows(syz) + forward_lanes(szz))

    everything = slice(None)

    def first_copies(dx, dy):
        if dx and dy:
            return []
        k = {(1, 0): 0, (-1, 0): 1, (0, 1): 2, (0, -1): 3}[dx, dy]
        here, into = {
            (1, 0): ((pl.ds(4, 2), pl.ds(2, 12)), (pl.ds(0, 2), pl.ds(2, 12))),
            (-1, 0): ((pl.ds(2, 2), pl.ds(2, 12)), (pl.ds(6, 2), pl.ds(2, 12))),
            (0, 1): ((pl.ds(2, 4), pl.ds(12, 2)), (pl.ds(2, 4), pl.ds(0, 2))),
            (0, -1): ((pl.ds(2, 4), pl.ds(2, 2)), (pl.ds(2, 4), pl.ds(14, 2))),
        }[dx, dy]
        pairs = [
            (V.at[(everything,) + here], V.at[(everything,) + into]),
            (CODE.at[here], CODE.at[into]),
        ]
        return [
            pltpu.make_async_remote_copy(
                src_ref=src,
                dst_ref=dst,
                send_sem=first_send.at[k, n],
                recv_sem=first_recv.at[k, n],
                device_id=(side[dx], along[dy]),
                device_id_type=MESH,
            )
            for n, (src, dst) in enumerate(pairs)
        ]

    def step_copies(t, dx, dy):
        slot = lax.rem(t, 2)
        plan = []
        if dx and dy:
            from_l, to_l = (6, 2) if dx == 1 else (0, 4)
            from_r, to_r = (12, 0) if dy == 1 else (2, 14)
            plan.append((everything, from_l, 2, from_r, 2, RA, to_l, to_r))
            from_l, to_l = (4, 0) if dx == 1 else (2, 6)
            from_r, to_r = (14, 2) if dy == 1 else (0, 12)
            plan.append((everything, from_l, 2, from_r, 2, RB, to_l, to_r))
        elif dy:
            from_r, to_r = (12, 0) if dy == 1 else (0, 12)
            plan.append((everything, 2, 4, from_r, 4, RB, 2, to_r))
        else:
            for c in range(3):
                from_l, to_l = (TO_HIGH if dx == 1 else TO_LOW)[c]
                plan.append((c, from_l, 3, 2, 12, RA, to_l, 2))
        k = around.index((dx, dy))
        return [
            pltpu.make_async_remote_copy(
                src_ref=G.at[c, pl.ds(from_l, n_l), pl.ds(from_r, n_r), :],
                dst_ref=ref.at[slot, c, pl.ds(to_l, n_l), pl.ds(to_r, n_r), :],
                send_sem=send_sem.at[slot, k, n],
                recv_sem=recv_sem.at[slot, k, n],
                device_id=(side[dx], along[dy]),
                device_id_type=MESH,
            )
            for n, (c, from_l, n_l, from_r, n_r, ref, to_l, to_r) in enumerate(plan)
        ]

    def start_all(copies_of):
        for dx, dy in around:

            @pl.when(there(dx, dy))
            def _():
                for copy in copies_of(dx, dy):
                    copy.start()

    def wait_all(copies_of, received):
        for dx, dy in around:

            @pl.when(there(-dx, -dy) if received else there(dx, dy))
            def _():
                for copy in copies_of(dx, dy):
                    if received:
                        copy.wait_recv()
                    else:
                        copy.wait_send()

    for load in loads[:4]:
        load.wait()
    forces()
    for load in loads[4:]:
        load.wait()

    n_x = 1 + has_x[1].astype(jnp.int32) + has_x[-1].astype(jnp.int32)
    n_y = 1 + has_y[1].astype(jnp.int32) + has_y[-1].astype(jnp.int32)
    pl.semaphore_wait(barrier, n_x * n_y - 1)
    start_all(functools.partial(step_copies, 0))
    start_all(first_copies)
    for load in small:
        load.wait()

    def look_up(code, r):
        values = [table[r, k] for k in range(16)]
        for bit in range(4):
            chosen = (code & (1 << bit)) != 0
            values = [
                jnp.where(chosen, values[2 * k + 1], values[2 * k])
                for k in range(len(values) // 2)
            ]
        return values[0]

    moduli = jnp.zeros((1, ROWS, 128), jnp.float32)
    for j in range(3):
        for k in range(128 // BLKZ):
            here = (
                (row >= 2 + BLK * j)
                & (row < 2 + BLK * (j + 1))
                & (lane >= BLKZ * k)
                & (lane < BLKZ * (k + 1))
            )
            moduli = jnp.where(here, scale[j, 0, k], moduli)
    code = CODE[2:6, 2:14]

    def keep(n, value):
        PROP[n, :, 2:14] = value

    own_moduli = moduli[:, 2:14]
    keep(0, look_up(code, 1) * own_moduli)
    keep(1, look_up(code, 2) * own_moduli)
    decay = look_up(code, 3)
    gain = (1.0 - decay) * look_up(code, 4)
    keep(2, decay)
    keep(3, gain)
    keep(4, time_step * (1.0 - 0.5 * gain))
    keep(5, (0.5 * time_step) * (1.0 + decay))
    keep(6, look_up(code, 5))

    cell = (
        (
            lax.broadcasted_iota(jnp.int32, block, 0) * 12
            + lax.broadcasted_iota(jnp.int32, block, 1)
            - 2
        )
        * 128
        + lax.broadcasted_iota(jnp.int32, block, 2)
    )
    for n in range(STEPS):
        added = jnp.zeros(block, jnp.float32)
        for k in range(4):
            added = added + jnp.where(
                cell == cells[0, 0, k], time_step * amps[0, 0, k, n], 0.0
            )
        SRC[n] = added

    wait_all(first_copies, True)
    wait_all(first_copies, False)

    layer = lax.broadcasted_iota(jnp.int32, (LAYERS, ROWS, 128), 0)
    rows = lax.broadcasted_iota(jnp.int32, (LAYERS, ROWS, 128), 1)
    inside = (
        (layer >= jnp.where(we == 0, 2, 0))
        & (layer < jnp.where(we == n_we - 1, 6, 8))
        & (rows >= jnp.where(sn == 0, 2, 0))
        & (rows < jnp.where(sn == n_sn - 1, 14, 16))
    )
    DB[...] = jnp.where(inside, time_step * look_up(CODE[...], 0), 0.0)
    for c in range(3):
        V[c] = jnp.where(inside, V[c], 0.0)

    v_stores = [
        pltpu.make_async_copy(V.at[:, 2 + x, 2:14, :], vel_out.at[:, :, x, :], load_sem.at[0, x])
        for x in range(4)
    ]

    def step(t, carry):
        copies = functools.partial(step_copies, t)
        slot = lax.rem(t, 2)
        wait_all(copies, True)

        for c in range(3):
            V[c] = V[c] + DB[...] * (G[c] + RA[slot, c] + RB[slot, c])

        @pl.when(t == STEPS - 1)
        def _():
            for store in v_stores:
                store.start()

        def forward_x(c):
            return inner_coef * (V[c, 3:7] - V[c, 2:6]) - outer_coef * (V[c, 4:8] - V[c, 1:5])

        def backward_x(c):
            return inner_coef * (V[c, 2:6] - V[c, 1:5]) - outer_coef * (V[c, 3:7] - V[c, 0:4])

        ve, vn, vd = (V[c, 2:6] for c in range(3))
        exx = backward_x(0)
        eyy = backward_rows(vn)
        ezz = backward_lanes(vd)
        exz = forward_lanes(ve) + forward_x(2)
        exy = forward_rows(ve) + forward_x(1)
        eyz = forward_lanes(vn) + forward_rows(vd)
        lame, shear = PROP[0], PROP[1]
        volume = lame * (exx + eyy + ezz)
        twice = shear + shear
        rates = (
            volume + twice * exx,
            shear * exz,
            shear * exy,
            shear * eyz,
            volume + twice * eyy,
            volume + twice * ezz,
        )
        trial = []
        for c in range(6):
            memory = M[c]
            M[c] = PROP[2] * memory + PROP[3] * rates[c]
            trial.append(S[c] + PROP[4] * rates[c] - PROP[5] * memory)
        added = SRC[t]
        for c in (0, 4, 5):
            trial[c] = trial[c] + added
        mean = (trial[0] + trial[4] + trial[5]) * (1.0 / 3.0)
        for c in (0, 4, 5):
            trial[c] = trial[c] - mean
        normal = trial[0] * trial[0] + trial[4] * trial[4] + trial[5] * trial[5]
        second = 0.5 * normal + (
            trial[1] * trial[1] + trial[2] * trial[2] + trial[3] * trial[3]
        )
        soft = jnp.maximum(-mean, 0.0) + ln_2 * jnp.log2(1.0 + jnp.exp2(-log2_e * jnp.abs(mean)))
        level = PROP[6] + friction * soft
        scaled = second / (level * level)
        factor = jnp.exp2(-0.25 * jnp.log2(1.0 + scaled * scaled))
        own = (row >= 2) & (row < 14)
        for c in range(6):
            new = factor * trial[c]
            if c in (0, 4, 5):
                new = mean + new
            S[c] = jnp.where(own, new, 0.0)

        wait_all(copies, False)

        @pl.when(t < STEPS - 1)
        def _():
            forces()
            start_all(functools.partial(step_copies, t + 1))

        return carry

    lax.fori_loop(0, STEPS, step, 0)

    stores = []
    for n, (src, dst) in enumerate(((S, str_out), (M, mem_out))):
        for x in range(4):
            stores.append(
                pltpu.make_async_copy(
                    src.at[:, x, 2:14, :], dst.at[:, :, x, :], load_sem.at[n + 1, x]
                )
            )
            stores[-1].start()
    for store in v_stores + stores:
        store.wait()


def solution(mesh):
    counts = (mesh.shape["we"], mesh.shape["sn"])
    f32 = jnp.float32

    def shards(velocity, stress, memory, code, scale, table, cells, amps):
        velocity, stress, memory = (
            jnp.transpose(a, (0, 2, 1, 3)) for a in (velocity, stress, memory)
        )
        code = jnp.transpose(code, (1, 0, 2))
        scale = jnp.transpose(scale, (1, 0, 2))
        hbm = pl.BlockSpec(memory_space=pltpu.HBM)
        outs = pl.pallas_call(
            functools.partial(kernel, counts),
            out_shape=tuple(
                jax.ShapeDtypeStruct(a.shape, f32) for a in (velocity, stress, memory)
            ),
            in_specs=[hbm] * 8,
            out_specs=(hbm,) * 3,
            scratch_shapes=[
                pltpu.VMEM((3, LAYERS, ROWS, 128), f32),
                pltpu.VMEM((6, 4, ROWS, 128), f32),
                pltpu.VMEM((6, 4, ROWS, 128), f32),
                pltpu.VMEM((LAYERS, ROWS, 128), jnp.int32),
                pltpu.VMEM((3, LAYERS, ROWS, 128), f32),
                pltpu.VMEM((2, 3, LAYERS, ROWS, 128), f32),
                pltpu.VMEM((2, 3, LAYERS, ROWS, 128), f32),
                pltpu.VMEM((LAYERS, ROWS, 128), f32),
                pltpu.VMEM((7, 4, ROWS, 128), f32),
                pltpu.VMEM((STEPS, 4, ROWS, 128), f32),
                pltpu.SMEM(scale.shape, f32),
                pltpu.SMEM(table.shape, f32),
                pltpu.SMEM(cells.shape, jnp.int32),
                pltpu.SMEM(amps.shape, f32),
                pltpu.SemaphoreType.DMA((4, 4)),
                pltpu.SemaphoreType.DMA((4,)),
                pltpu.SemaphoreType.DMA((4, 2)),
                pltpu.SemaphoreType.DMA((4, 2)),
                pltpu.SemaphoreType.DMA((2, 8, 3)),
                pltpu.SemaphoreType.DMA((2, 8, 3)),
            ],
            compiler_params=pltpu.CompilerParams(
                collective_id=0, has_side_effects=True, vmem_limit_bytes=62 * 1024 * 1024
            ),
        )(velocity, stress, memory, code, scale, table, cells, amps)
        return tuple(jnp.transpose(a, (0, 2, 1, 3)) for a in outs)

    in_specs = (
        P(None, "we", "sn", None),
        P(None, "we", "sn", None),
        P(None, "we", "sn", None),
        P("we", "sn", None),
        P("we", "sn", None),
        P(),
        P("we", "sn", None),
        P("we", "sn", None, None),
    )
    out_specs = (P(None, "we", "sn", None),) * 3
    return jax.shard_map(shards, mesh=mesh, in_specs=in_specs, out_specs=out_specs, check_vma=False)
```

```python
import functools

import jax
import jax.numpy as jnp
from jax import lax
from jax.experimental import pallas as pl
from jax.experimental.pallas import tpu as pltpu
from jax.sharding import PartitionSpec as P

STEPS = 4
BLK = 4
BLKZ = 32
MESH = pl.DeviceIdType.MESH

inner_coef = 9.0 / 8.0
outer_coef = 1.0 / 24.0
time_step = 0.08
friction = 0.4
log2_e = 1.4426950408889634
ln_2 = 0.6931471805599453

LAYERS = 8
ROWS = 16

TO_HIGH = ((4, 0), (5, 1), (5, 1))
TO_LOW = ((0, 4), (1, 5), (1, 5))


def forward(layers, i):
    return combine(layers, (i + 1, i, i + 2, i - 1))


def backward(layers, i):
    return combine(layers, (i, i - 1, i + 1, i - 2))


def combine(layers, at):
    terms = []
    for index, coef in zip(at, (inner_coef, -inner_coef, -outer_coef, outer_coef)):
        if 0 <= index < len(layers):
            terms.append((coef, layers[index]))
    total = None
    for coef, layer in terms:
        total = coef * layer if total is None else total + coef * layer
    return total


def moved(field, offset, axis):
    size = field.shape[axis]
    return pltpu.roll(field, (-offset) % size, axis)


def forward_rows(field):
    return inner_coef * (moved(field, 1, 1) - field) - outer_coef * (
        moved(field, 2, 1) - moved(field, -1, 1)
    )


def backward_rows(field):
    return inner_coef * (field - moved(field, -1, 1)) - outer_coef * (
        moved(field, 1, 1) - moved(field, -2, 1)
    )


def kernel(
    counts,
    vel_in,
    str_in,
    mem_in,
    code_in,
    scale_in,
    table_in,
    cells_in,
    amps_in,
    V,
    S,
    M,
    CODE,
    G,
    RA,
    RB,
    DB,
    PROP,
    SRC,
    scale,
    table,
    cells,
    amps,
    load_sem,
    small_sem,
    first_send,
    first_recv,
    send_sem,
    recv_sem,
):
    n_we, n_sn = counts
    we = lax.axis_index("we")
    sn = lax.axis_index("sn")
    side = {
        0: we,
        1: jnp.minimum(we + 1, n_we - 1),
        -1: jnp.maximum(we - 1, 0),
    }
    along = {
        0: sn,
        1: jnp.minimum(sn + 1, n_sn - 1),
        -1: jnp.maximum(sn - 1, 0),
    }
    has_x = {1: we < n_we - 1, -1: we > 0}
    has_y = {1: sn < n_sn - 1, -1: sn > 0}

    def there(dx, dy):
        if dx and dy:
            return has_x[dx] & has_y[dy]
        return has_x[dx] if dx else has_y[dy]

    around = [(dx, dy) for dx in (1, -1) for dy in (1, -1)]
    around += [(0, 1), (0, -1), (1, 0), (-1, 0)]

    RA[0] = jnp.zeros((3, LAYERS, ROWS, 128), jnp.float32)
    RB[0] = jnp.zeros((3, LAYERS, ROWS, 128), jnp.float32)

    barrier = pltpu.get_barrier_semaphore()
    for dx, dy in around:

        @pl.when(there(dx, dy))
        def _():
            pl.semaphore_signal(
                barrier, inc=1, device_id=(side[dx], along[dy]), device_id_type=MESH
            )

    loads = []
    for n, (src, dst, first) in enumerate(((str_in, S, 0), (code_in, CODE, 2), (vel_in, V, 2), (mem_in, M, 0))):
        for x in range(4):
            if src is code_in:
                pair = src.at[:, x, :], dst.at[first + x, 2:14, :]
            else:
                pair = src.at[:, :, x, :], dst.at[:, first + x, 2:14, :]
            loads.append(pltpu.make_async_copy(*pair, load_sem.at[n, x]))
            loads[-1].start()
    small = [
        pltpu.make_async_copy(src, dst, small_sem.at[n])
        for n, (src, dst) in enumerate(
            ((scale_in, scale), (table_in, table), (cells_in, cells), (amps_in, amps))
        )
    ]
    for load in small:
        load.start()

    edge_rows = jnp.zeros((6, 4, 2, 128), jnp.float32)
    S[:, :, 0:2, :] = edge_rows
    S[:, :, 14:16, :] = edge_rows
    G[0, 7] = jnp.zeros((ROWS, 128), jnp.float32)
    G[1, 0] = jnp.zeros((ROWS, 128), jnp.float32)
    G[2, 0] = jnp.zeros((ROWS, 128), jnp.float32)
    RA[1] = jnp.zeros((3, LAYERS, ROWS, 128), jnp.float32)
    RB[1] = jnp.zeros((3, LAYERS, ROWS, 128), jnp.float32)

    block = (4, ROWS, 128)
    lane = lax.broadcasted_iota(jnp.int32, (1, 1, 128), 2)
    row = lax.broadcasted_iota(jnp.int32, (1, ROWS, 128), 1)

    def lane_coef(coef, offset):
        inside = (lane + offset >= 0) & (lane + offset < 128)
        return jnp.where(inside, coef, 0.0)

    def forward_lanes(field):
        return (
            lane_coef(inner_coef, 1) * moved(field, 1, 2)
            - inner_coef * field
            - lane_coef(outer_coef, 2) * moved(field, 2, 2)
            + lane_coef(outer_coef, -1) * moved(field, -1, 2)
        )

    def backward_lanes(field):
        return (
            inner_coef * field
            - lane_coef(inner_coef, -1) * moved(field, -1, 2)
            - lane_coef(outer_coef, 1) * moved(field, 1, 2)
            + lane_coef(outer_coef, -2) * moved(field, -2, 2)
        )

    def force(component, along_x, field_x, rest):
        layers = [field_x[i] for i in range(4)]
        for i in range(-2, 6):
            part = along_x(layers, i)
            if part is None:
                continue
            if 0 <= i < 4:
                part = part + rest[i]
            G[component, i + 2] = part

    def forces():
        sxx, sxz, sxy, syz, syy, szz = (S[c] for c in range(6))
        force(0, forward, sxx, backward_rows(sxy) + backward_lanes(sxz))
        force(1, backward, sxy, forward_rows(syy) + backward_lanes(syz))
        force(2, backward, sxz, backward_rows(syz) + forward_lanes(szz))

    everything = slice(None)

    def first_copies(dx, dy):
        if dx and dy:
            return []
        k = {(1, 0): 0, (-1, 0): 1, (0, 1): 2, (0, -1): 3}[dx, dy]
        here, into = {
            (1, 0): ((pl.ds(4, 2), pl.ds(2, 12)), (pl.ds(0, 2), pl.ds(2, 12))),
            (-1, 0): ((pl.ds(2, 2), pl.ds(2, 12)), (pl.ds(6, 2), pl.ds(2, 12))),
            (0, 1): ((pl.ds(2, 4), pl.ds(12, 2)), (pl.ds(2, 4), pl.ds(0, 2))),
            (0, -1): ((pl.ds(2, 4), pl.ds(2, 2)), (pl.ds(2, 4), pl.ds(14, 2))),
        }[dx, dy]
        pairs = [
            (V.at[(everything,) + here], V.at[(everything,) + into]),
            (CODE.at[here], CODE.at[into]),
        ]
        return [
            pltpu.make_async_remote_copy(
                src_ref=src,
                dst_ref=dst,
                send_sem=first_send.at[k, n],
                recv_sem=first_recv.at[k, n],
                device_id=(side[dx], along[dy]),
                device_id_type=MESH,
            )
            for n, (src, dst) in enumerate(pairs)
        ]

    def step_copies(t, dx, dy):
        slot = lax.rem(t, 2)
        plan = []
        if dx and dy:
            from_l, to_l = (6, 2) if dx == 1 else (0, 4)
            from_r, to_r = (12, 0) if dy == 1 else (2, 14)
            plan.append((everything, from_l, 2, from_r, 2, RA, to_l, to_r))
            from_l, to_l = (4, 0) if dx == 1 else (2, 6)
            from_r, to_r = (14, 2) if dy == 1 else (0, 12)
            plan.append((everything, from_l, 2, from_r, 2, RB, to_l, to_r))
        elif dy:
            from_r, to_r = (12, 0) if dy == 1 else (0, 12)
            plan.append((everything, 2, 4, from_r, 4, RB, 2, to_r))
        else:
            for c in range(3):
                from_l, to_l = (TO_HIGH if dx == 1 else TO_LOW)[c]
                plan.append((c, from_l, 3, 2, 12, RA, to_l, 2))
        k = around.index((dx, dy))
        return [
            pltpu.make_async_remote_copy(
                src_ref=G.at[c, pl.ds(from_l, n_l), pl.ds(from_r, n_r), :],
                dst_ref=ref.at[slot, c, pl.ds(to_l, n_l), pl.ds(to_r, n_r), :],
                send_sem=send_sem.at[slot, k, n],
                recv_sem=recv_sem.at[slot, k, n],
                device_id=(side[dx], along[dy]),
                device_id_type=MESH,
            )
            for n, (c, from_l, n_l, from_r, n_r, ref, to_l, to_r) in enumerate(plan)
        ]

    def start_all(copies_of):
        for dx, dy in around:

            @pl.when(there(dx, dy))
            def _():
                for copy in copies_of(dx, dy):
                    copy.start()

    def wait_all(copies_of, received):
        for dx, dy in around:

            @pl.when(there(-dx, -dy) if received else there(dx, dy))
            def _():
                for copy in copies_of(dx, dy):
                    if received:
                        copy.wait_recv()
                    else:
                        copy.wait_send()

    for load in loads[:4]:
        load.wait()
    forces()
    for load in loads[4:]:
        load.wait()

    n_x = 1 + has_x[1].astype(jnp.int32) + has_x[-1].astype(jnp.int32)
    n_y = 1 + has_y[1].astype(jnp.int32) + has_y[-1].astype(jnp.int32)
    pl.semaphore_wait(barrier, n_x * n_y - 1)
    start_all(functools.partial(step_copies, 0))
    start_all(first_copies)
    for load in small:
        load.wait()

    def look_up(code, r):
        values = [table[r, k] for k in range(16)]
        for bit in range(4):
            chosen = (code & (1 << bit)) != 0
            values = [
                jnp.where(chosen, values[2 * k + 1], values[2 * k])
                for k in range(len(values) // 2)
            ]
        return values[0]

    moduli = jnp.zeros((1, ROWS, 128), jnp.float32)
    for j in range(3):
        for k in range(128 // BLKZ):
            here = (
                (row >= 2 + BLK * j)
                & (row < 2 + BLK * (j + 1))
                & (lane >= BLKZ * k)
                & (lane < BLKZ * (k + 1))
            )
            moduli = jnp.where(here, scale[j, 0, k], moduli)
    code = CODE[2:6, 2:14]

    def keep(n, value):
        PROP[n, :, 2:14] = value

    own_moduli = moduli[:, 2:14]
    keep(0, look_up(code, 1) * own_moduli)
    keep(1, look_up(code, 2) * own_moduli)
    decay = look_up(code, 3)
    gain = (1.0 - decay) * look_up(code, 4)
    keep(2, decay)
    keep(3, gain)
    keep(4, time_step * (1.0 - 0.5 * gain))
    keep(5, (0.5 * time_step) * (1.0 + decay))
    keep(6, look_up(code, 5))

    cell = (
        (
            lax.broadcasted_iota(jnp.int32, block, 0) * 12
            + lax.broadcasted_iota(jnp.int32, block, 1)
            - 2
        )
        * 128
        + lax.broadcasted_iota(jnp.int32, block, 2)
    )
    for n in range(STEPS):
        added = jnp.zeros(block, jnp.float32)
        for k in range(4):
            added = added + jnp.where(
                cell == cells[0, 0, k], time_step * amps[0, 0, k, n], 0.0
            )
        SRC[n] = added

    wait_all(first_copies, True)
    wait_all(first_copies, False)

    layer = lax.broadcasted_iota(jnp.int32, (LAYERS, ROWS, 128), 0)
    rows = lax.broadcasted_iota(jnp.int32, (LAYERS, ROWS, 128), 1)
    inside = (
        (layer >= jnp.where(we == 0, 2, 0))
        & (layer < jnp.where(we == n_we - 1, 6, 8))
        & (rows >= jnp.where(sn == 0, 2, 0))
        & (rows < jnp.where(sn == n_sn - 1, 14, 16))
    )
    DB[...] = jnp.where(inside, time_step * look_up(CODE[...], 0), 0.0)
    for c in range(3):
        V[c] = jnp.where(inside, V[c], 0.0)

    def step(t, carry):
        copies = functools.partial(step_copies, t)
        slot = lax.rem(t, 2)
        wait_all(copies, True)

        for c in range(3):
            V[c] = V[c] + DB[...] * (G[c] + RA[slot, c] + RB[slot, c])

        def forward_x(c):
            return inner_coef * (V[c, 3:7] - V[c, 2:6]) - outer_coef * (V[c, 4:8] - V[c, 1:5])

        def backward_x(c):
            return inner_coef * (V[c, 2:6] - V[c, 1:5]) - outer_coef * (V[c, 3:7] - V[c, 0:4])

        ve, vn, vd = (V[c, 2:6] for c in range(3))
        exx = backward_x(0)
        eyy = backward_rows(vn)
        ezz = backward_lanes(vd)
        exz = forward_lanes(ve) + forward_x(2)
        exy = forward_rows(ve) + forward_x(1)
        eyz = forward_lanes(vn) + forward_rows(vd)
        lame, shear = PROP[0], PROP[1]
        volume = lame * (exx + eyy + ezz)
        twice = shear + shear
        rates = (
            volume + twice * exx,
            shear * exz,
            shear * exy,
            shear * eyz,
            volume + twice * eyy,
            volume + twice * ezz,
        )
        trial = []
        for c in range(6):
            memory = M[c]
            M[c] = PROP[2] * memory + PROP[3] * rates[c]
            trial.append(S[c] + PROP[4] * rates[c] - PROP[5] * memory)
        added = SRC[t]
        for c in (0, 4, 5):
            trial[c] = trial[c] + added
        mean = (trial[0] + trial[4] + trial[5]) * (1.0 / 3.0)
        for c in (0, 4, 5):
            trial[c] = trial[c] - mean
        normal = trial[0] * trial[0] + trial[4] * trial[4] + trial[5] * trial[5]
        second = 0.5 * normal + (
            trial[1] * trial[1] + trial[2] * trial[2] + trial[3] * trial[3]
        )
        soft = jnp.maximum(-mean, 0.0) + ln_2 * jnp.log2(1.0 + jnp.exp2(-log2_e * jnp.abs(mean)))
        level = PROP[6] + friction * soft
        scaled = second / (level * level)
        factor = jnp.exp2(-0.25 * jnp.log2(1.0 + scaled * scaled))
        own = (row >= 2) & (row < 14)
        for c in range(6):
            new = factor * trial[c]
            if c in (0, 4, 5):
                new = mean + new
            S[c] = jnp.where(own, new, 0.0)

        wait_all(copies, False)

        @pl.when(t < STEPS - 1)
        def _():
            forces()
            start_all(functools.partial(step_copies, t + 1))

        return carry

    lax.fori_loop(0, STEPS, step, 0)


def write_out(V, S, M, vel_out, str_out, mem_out, sem):
    stores = []
    for n, (src, first, dst) in enumerate(((V, 2, vel_out), (S, 0, str_out), (M, 0, mem_out))):
        for x in range(4):
            stores.append(
                pltpu.make_async_copy(
                    src.at[:, first + x, pl.ds(2, 12), :], dst.at[:, :, x, :], sem.at[n, x]
                )
            )
            stores[-1].start()
    for store in stores:
        store.wait()


def solution(mesh):
    counts = (mesh.shape["we"], mesh.shape["sn"])
    f32 = jnp.float32

    def shards(velocity, stress, memory, code, scale, table, cells, amps):
        velocity, stress, memory = (
            jnp.transpose(a, (0, 2, 1, 3)) for a in (velocity, stress, memory)
        )
        code = jnp.transpose(code, (1, 0, 2))
        scale = jnp.transpose(scale, (1, 0, 2))
        hbm = pl.BlockSpec(memory_space=pltpu.HBM)
        operands = [
            pltpu.with_memory_space_constraint(a, pltpu.HBM)
            for a in (velocity, stress, memory, code, scale, table, cells, amps)
        ]
        vmem = pl.BlockSpec(memory_space=pltpu.VMEM)
        fields = pl.pallas_call(
            functools.partial(kernel, counts),
            out_shape=(
                pltpu.VMEM((3, LAYERS, ROWS, 128), f32),
                pltpu.VMEM((6, 4, ROWS, 128), f32),
                pltpu.VMEM((6, 4, ROWS, 128), f32),
            ),
            in_specs=[hbm] * 8,
            out_specs=(vmem,) * 3,
            scratch_shapes=[
                pltpu.VMEM((LAYERS, ROWS, 128), jnp.int32),
                pltpu.VMEM((3, LAYERS, ROWS, 128), f32),
                pltpu.VMEM((2, 3, LAYERS, ROWS, 128), f32),
                pltpu.VMEM((2, 3, LAYERS, ROWS, 128), f32),
                pltpu.VMEM((LAYERS, ROWS, 128), f32),
                pltpu.VMEM((7, 4, ROWS, 128), f32),
                pltpu.VMEM((STEPS, 4, ROWS, 128), f32),
                pltpu.SMEM(scale.shape, f32),
                pltpu.SMEM(table.shape, f32),
                pltpu.SMEM(cells.shape, jnp.int32),
                pltpu.SMEM(amps.shape, f32),
                pltpu.SemaphoreType.DMA((4, 4)),
                pltpu.SemaphoreType.DMA((4,)),
                pltpu.SemaphoreType.DMA((4, 2)),
                pltpu.SemaphoreType.DMA((4, 2)),
                pltpu.SemaphoreType.DMA((2, 8, 3)),
                pltpu.SemaphoreType.DMA((2, 8, 3)),
            ],
            compiler_params=pltpu.CompilerParams(
                collective_id=0, has_side_effects=True, vmem_limit_bytes=16 * 1024 * 1024
            ),
        )(*operands)
        outs = pl.pallas_call(
            write_out,
            out_shape=tuple(
                jax.ShapeDtypeStruct(a.shape, f32) for a in (velocity, stress, memory)
            ),
            in_specs=[vmem] * 3,
            out_specs=(hbm,) * 3,
            scratch_shapes=[pltpu.SemaphoreType.DMA((3, 4))],
            compiler_params=pltpu.CompilerParams(vmem_limit_bytes=4 * 1024 * 1024),
        )(*(pltpu.with_memory_space_constraint(a, pltpu.VMEM) for a in fields))
        return tuple(jnp.transpose(a, (0, 2, 1, 3)) for a in outs)

    in_specs = (
        P(None, "we", "sn", None),
        P(None, "we", "sn", None),
        P(None, "we", "sn", None),
        P("we", "sn", None),
        P("we", "sn", None),
        P(),
        P("we", "sn", None),
        P("we", "sn", None, None),
    )
    out_specs = (P(None, "we", "sn", None),) * 3
    return jax.shard_map(shards, mesh=mesh, in_specs=in_specs, out_specs=out_specs, check_vma=False)
```

```python
import functools

import jax
import jax.numpy as jnp
from jax import lax
from jax.experimental import pallas as pl
from jax.experimental.pallas import tpu as pltpu
from jax.sharding import PartitionSpec as P

STEPS = 4
BLK = 4
BLKZ = 32
MESH = pl.DeviceIdType.MESH

inner_coef = 9.0 / 8.0
outer_coef = 1.0 / 24.0
time_step = 0.08
friction = 0.4
log2_e = 1.4426950408889634
ln_2 = 0.6931471805599453

LAYERS = 8
ROWS = 16

TO_HIGH = ((4, 0), (5, 1), (5, 1))
TO_LOW = ((0, 4), (1, 5), (1, 5))


def forward(layers, i):
    return combine(layers, (i + 1, i, i + 2, i - 1))


def backward(layers, i):
    return combine(layers, (i, i - 1, i + 1, i - 2))


def combine(layers, at):
    terms = []
    for index, coef in zip(at, (inner_coef, -inner_coef, -outer_coef, outer_coef)):
        if 0 <= index < len(layers):
            terms.append((coef, layers[index]))
    total = None
    for coef, layer in terms:
        total = coef * layer if total is None else total + coef * layer
    return total


def moved(field, offset, axis):
    size = field.shape[axis]
    return pltpu.roll(field, (-offset) % size, axis)


def forward_rows(field):
    return inner_coef * (moved(field, 1, 1) - field) - outer_coef * (
        moved(field, 2, 1) - moved(field, -1, 1)
    )


def backward_rows(field):
    return inner_coef * (field - moved(field, -1, 1)) - outer_coef * (
        moved(field, 1, 1) - moved(field, -2, 1)
    )


def kernel(
    counts,
    vel_in,
    str_in,
    mem_in,
    code_in,
    scale_in,
    table_in,
    cells_in,
    amps_in,
    V,
    S,
    M,
    CODE,
    G,
    GY,
    RA,
    RB,
    DB,
    PROP,
    SRC,
    scale,
    table,
    cells,
    amps,
    load_sem,
    small_sem,
    first_send,
    first_recv,
    send_sem,
    recv_sem,
):
    n_we, n_sn = counts
    we = lax.axis_index("we")
    sn = lax.axis_index("sn")
    side = {
        0: we,
        1: jnp.minimum(we + 1, n_we - 1),
        -1: jnp.maximum(we - 1, 0),
    }
    along_sn = {
        0: sn,
        1: jnp.minimum(sn + 1, n_sn - 1),
        -1: jnp.maximum(sn - 1, 0),
    }
    has_x = {1: we < n_we - 1, -1: we > 0}
    has_y = {1: sn < n_sn - 1, -1: sn > 0}

    def there(dx, dy):
        if dx and dy:
            return has_x[dx] & has_y[dy]
        return has_x[dx] if dx else has_y[dy]

    around = [(dx, dy) for dx in (1, -1) for dy in (1, -1)]
    around += [(0, 1), (0, -1), (1, 0), (-1, 0)]

    RA[0] = jnp.zeros((3, LAYERS, ROWS, 128), jnp.float32)
    RB[0] = jnp.zeros((3, LAYERS, ROWS, 128), jnp.float32)

    barrier = pltpu.get_barrier_semaphore()
    for dx, dy in around:

        @pl.when(there(dx, dy))
        def _():
            pl.semaphore_signal(
                barrier, inc=1, device_id=(side[dx], along_sn[dy]), device_id_type=MESH
            )

    loads = []
    for n, (src, dst, first) in enumerate(((str_in, S, 0), (code_in, CODE, 2), (vel_in, V, 2), (mem_in, M, 0))):
        for x in range(4):
            if src is code_in:
                pair = src.at[:, x, :], dst.at[first + x, 2:14, :]
            else:
                pair = src.at[:, :, x, :], dst.at[:, first + x, 2:14, :]
            loads.append(pltpu.make_async_copy(*pair, load_sem.at[n, x]))
            loads[-1].start()
    small = [
        pltpu.make_async_copy(src, dst, small_sem.at[n])
        for n, (src, dst) in enumerate(
            ((scale_in, scale), (table_in, table), (cells_in, cells), (amps_in, amps))
        )
    ]
    for load in small:
        load.start()

    edge_rows = jnp.zeros((6, 4, 2, 128), jnp.float32)
    S[:, :, 0:2, :] = edge_rows
    S[:, :, 14:16, :] = edge_rows
    G[0, 7] = jnp.zeros((ROWS, 128), jnp.float32)
    G[1, 0] = jnp.zeros((ROWS, 128), jnp.float32)
    G[2, 0] = jnp.zeros((ROWS, 128), jnp.float32)
    RA[1] = jnp.zeros((3, LAYERS, ROWS, 128), jnp.float32)
    RB[1] = jnp.zeros((3, LAYERS, ROWS, 128), jnp.float32)

    block = (4, ROWS, 128)
    lane = lax.broadcasted_iota(jnp.int32, (1, 1, 128), 2)
    row = lax.broadcasted_iota(jnp.int32, (1, ROWS, 128), 1)

    def lane_coef(coef, offset):
        inside = (lane + offset >= 0) & (lane + offset < 128)
        return jnp.where(inside, coef, 0.0)

    def forward_lanes(field):
        return (
            lane_coef(inner_coef, 1) * moved(field, 1, 2)
            - inner_coef * field
            - lane_coef(outer_coef, 2) * moved(field, 2, 2)
            + lane_coef(outer_coef, -1) * moved(field, -1, 2)
        )

    def backward_lanes(field):
        return (
            inner_coef * field
            - lane_coef(inner_coef, -1) * moved(field, -1, 2)
            - lane_coef(outer_coef, 1) * moved(field, 1, 2)
            + lane_coef(outer_coef, -2) * moved(field, -2, 2)
        )

    along = (forward, backward, backward)
    along_field = (0, 2, 1)

    def rim_forces():
        sxy, syz, syy = S[2], S[3], S[4]
        GY[0] = backward_rows(sxy)
        GY[1] = forward_rows(syy)
        GY[2] = backward_rows(syz)
        for c in range(3):
            layers = [S[along_field[c], x] for x in range(4)]
            for i in (-2, -1, 4, 5):
                part = along[c](layers, i)
                if part is not None:
                    G[c, i + 2] = part

    def own_forces():
        depth = (backward_lanes(S[1]), backward_lanes(S[3]), forward_lanes(S[5]))
        for c in range(3):
            layers = [S[along_field[c], x] for x in range(4)]
            rest = GY[c] + depth[c]
            for i in range(4):
                G[c, i + 2] = along[c](layers, i) + rest[i]

    everything = slice(None)

    def first_copies(dx, dy):
        if dx and dy:
            return []
        k = {(1, 0): 0, (-1, 0): 1, (0, 1): 2, (0, -1): 3}[dx, dy]
        here, into = {
            (1, 0): ((pl.ds(4, 2), pl.ds(2, 12)), (pl.ds(0, 2), pl.ds(2, 12))),
            (-1, 0): ((pl.ds(2, 2), pl.ds(2, 12)), (pl.ds(6, 2), pl.ds(2, 12))),
            (0, 1): ((pl.ds(2, 4), pl.ds(12, 2)), (pl.ds(2, 4), pl.ds(0, 2))),
            (0, -1): ((pl.ds(2, 4), pl.ds(2, 2)), (pl.ds(2, 4), pl.ds(14, 2))),
        }[dx, dy]
        pairs = [
            (V.at[(everything,) + here], V.at[(everything,) + into]),
            (CODE.at[here], CODE.at[into]),
        ]
        return [
            pltpu.make_async_remote_copy(
                src_ref=src,
                dst_ref=dst,
                send_sem=first_send.at[k, n],
                recv_sem=first_recv.at[k, n],
                device_id=(side[dx], along_sn[dy]),
                device_id_type=MESH,
            )
            for n, (src, dst) in enumerate(pairs)
        ]

    def step_copies(t, dx, dy):
        slot = lax.rem(t, 2)
        plan = []
        if dx and dy:
            from_l, to_l = (6, 2) if dx == 1 else (0, 4)
            from_r, to_r = (12, 0) if dy == 1 else (2, 14)
            plan.append((G, everything, from_l, 2, from_r, 2, RA, to_l, to_r))
            from_l, to_l = (2, 0) if dx == 1 else (0, 6)
            from_r, to_r = (14, 2) if dy == 1 else (0, 12)
            plan.append((GY, everything, from_l, 2, from_r, 2, RB, to_l, to_r))
        elif dy:
            from_r, to_r = (12, 0) if dy == 1 else (0, 12)
            plan.append((G, everything, 2, 4, from_r, 4, RB, 2, to_r))
        else:
            for c in range(3):
                from_l, to_l = (TO_HIGH if dx == 1 else TO_LOW)[c]
                plan.append((G, c, from_l, 3, 2, 12, RA, to_l, 2))
        k = around.index((dx, dy))
        return [
            pltpu.make_async_remote_copy(
                src_ref=field.at[c, pl.ds(from_l, n_l), pl.ds(from_r, n_r), :],
                dst_ref=ref.at[slot, c, pl.ds(to_l, n_l), pl.ds(to_r, n_r), :],
                send_sem=send_sem.at[slot, k, n],
                recv_sem=recv_sem.at[slot, k, n],
                device_id=(side[dx], along_sn[dy]),
                device_id_type=MESH,
            )
            for n, (field, c, from_l, n_l, from_r, n_r, ref, to_l, to_r) in enumerate(plan)
        ]

    diagonal, sides = around[:4], around[4:]

    def start_all(copies_of, which):
        for dx, dy in which:

            @pl.when(there(dx, dy))
            def _():
                for copy in copies_of(dx, dy):
                    copy.start()

    def wait_all(copies_of, which, received):
        for dx, dy in which:

            @pl.when(there(-dx, -dy) if received else there(dx, dy))
            def _():
                for copy in copies_of(dx, dy):
                    if received:
                        copy.wait_recv()
                    else:
                        copy.wait_send()

    for load in loads[:4]:
        load.wait()
    rim_forces()
    own_forces()
    for load in loads[4:]:
        load.wait()

    n_x = 1 + has_x[1].astype(jnp.int32) + has_x[-1].astype(jnp.int32)
    n_y = 1 + has_y[1].astype(jnp.int32) + has_y[-1].astype(jnp.int32)
    pl.semaphore_wait(barrier, n_x * n_y - 1)
    start_all(functools.partial(step_copies, 0), around)
    start_all(first_copies, sides)
    for load in small:
        load.wait()

    def look_up(code, r):
        values = [table[r, k] for k in range(16)]
        for bit in range(4):
            chosen = (code & (1 << bit)) != 0
            values = [
                jnp.where(chosen, values[2 * k + 1], values[2 * k])
                for k in range(len(values) // 2)
            ]
        return values[0]

    moduli = jnp.zeros((1, ROWS, 128), jnp.float32)
    for j in range(3):
        for k in range(128 // BLKZ):
            here = (
                (row >= 2 + BLK * j)
                & (row < 2 + BLK * (j + 1))
                & (lane >= BLKZ * k)
                & (lane < BLKZ * (k + 1))
            )
            moduli = jnp.where(here, scale[j, 0, k], moduli)
    code = CODE[2:6, 2:14]

    def keep(n, value):
        PROP[n, :, 2:14] = value

    own_moduli = moduli[:, 2:14]
    keep(0, look_up(code, 1) * own_moduli)
    keep(1, look_up(code, 2) * own_moduli)
    decay = look_up(code, 3)
    gain = (1.0 - decay) * look_up(code, 4)
    keep(2, decay)
    keep(3, gain)
    keep(4, time_step * (1.0 - 0.5 * gain))
    keep(5, (0.5 * time_step) * (1.0 + decay))
    keep(6, look_up(code, 5))

    cell = (
        (
            lax.broadcasted_iota(jnp.int32, block, 0) * 12
            + lax.broadcasted_iota(jnp.int32, block, 1)
            - 2
        )
        * 128
        + lax.broadcasted_iota(jnp.int32, block, 2)
    )
    for n in range(STEPS):
        added = jnp.zeros(block, jnp.float32)
        for k in range(4):
            added = added + jnp.where(
                cell == cells[0, 0, k], time_step * amps[0, 0, k, n], 0.0
            )
        SRC[n] = added

    wait_all(first_copies, sides, True)
    wait_all(first_copies, sides, False)

    layer = lax.broadcasted_iota(jnp.int32, (LAYERS, ROWS, 128), 0)
    rows = lax.broadcasted_iota(jnp.int32, (LAYERS, ROWS, 128), 1)
    inside = (
        (layer >= jnp.where(we == 0, 2, 0))
        & (layer < jnp.where(we == n_we - 1, 6, 8))
        & (rows >= jnp.where(sn == 0, 2, 0))
        & (rows < jnp.where(sn == n_sn - 1, 14, 16))
    )
    DB[...] = jnp.where(inside, time_step * look_up(CODE[...], 0), 0.0)
    for c in range(3):
        V[c] = jnp.where(inside, V[c], 0.0)

    def step(t, carry):
        copies = functools.partial(step_copies, t)
        slot = lax.rem(t, 2)

        def advance(c, layers, rows):
            at = (layers, rows)
            arrived = RA[(slot, c) + at] + RB[(slot, c) + at]
            V[(c,) + at] = V[(c,) + at] + DB[at] * (G[(c,) + at] + arrived)

        wait_all(copies, sides, True)
        for c in range(3):
            advance(c, slice(2, 6), slice(2, 14))
        depth_of = (
            forward_lanes(V[0, 2:6]),
            forward_lanes(V[1, 2:6]),
            backward_lanes(V[2, 2:6]),
        )
        wait_all(copies, diagonal, True)
        for c in range(3):
            advance(c, slice(2, 6), slice(0, 2))
            advance(c, slice(2, 6), slice(14, 16))
            advance(c, slice(0, 2), slice(0, 16))
            advance(c, slice(6, 8), slice(0, 16))

        def forward_x(c):
            return inner_coef * (V[c, 3:7] - V[c, 2:6]) - outer_coef * (V[c, 4:8] - V[c, 1:5])

        def backward_x(c):
            return inner_coef * (V[c, 2:6] - V[c, 1:5]) - outer_coef * (V[c, 3:7] - V[c, 0:4])

        ve, vn, vd = (V[c, 2:6] for c in range(3))
        exx = backward_x(0)
        eyy = backward_rows(vn)
        ezz = depth_of[2]
        exz = depth_of[0] + forward_x(2)
        exy = forward_rows(ve) + forward_x(1)
        eyz = depth_of[1] + forward_rows(vd)
        lame, shear = PROP[0], PROP[1]
        volume = lame * (exx + eyy + ezz)
        twice = shear + shear
        rates = (
            volume + twice * exx,
            shear * exz,
            shear * exy,
            shear * eyz,
            volume + twice * eyy,
            volume + twice * ezz,
        )
        trial = []
        for c in range(6):
            memory = M[c]
            M[c] = PROP[2] * memory + PROP[3] * rates[c]
            trial.append(S[c] + PROP[4] * rates[c] - PROP[5] * memory)
        added = SRC[t]
        for c in (0, 4, 5):
            trial[c] = trial[c] + added
        mean = (trial[0] + trial[4] + trial[5]) * (1.0 / 3.0)
        for c in (0, 4, 5):
            trial[c] = trial[c] - mean
        normal = trial[0] * trial[0] + trial[4] * trial[4] + trial[5] * trial[5]
        second = 0.5 * normal + (
            trial[1] * trial[1] + trial[2] * trial[2] + trial[3] * trial[3]
        )
        soft = jnp.maximum(-mean, 0.0) + ln_2 * jnp.log2(1.0 + jnp.exp2(-log2_e * jnp.abs(mean)))
        level = PROP[6] + friction * soft
        scaled = second / (level * level)
        factor = jnp.exp2(-0.25 * jnp.log2(1.0 + scaled * scaled))
        own = (row >= 2) & (row < 14)
        for c in range(6):
            new = factor * trial[c]
            if c in (0, 4, 5):
                new = mean + new
            S[c] = jnp.where(own, new, 0.0)

        wait_all(copies, around, False)

        @pl.when(t < STEPS - 1)
        def _():
            later = functools.partial(step_copies, t + 1)
            rim_forces()
            start_all(later, diagonal)
            own_forces()
            start_all(later, sides)

        return carry

    lax.fori_loop(0, STEPS, step, 0)


def write_out(V, S, M, vel_out, str_out, mem_out, sem):
    stores = []
    for n, (src, first, dst) in enumerate(((V, 2, vel_out), (S, 0, str_out), (M, 0, mem_out))):
        for x in range(4):
            stores.append(
                pltpu.make_async_copy(
                    src.at[:, first + x, pl.ds(2, 12), :], dst.at[:, :, x, :], sem.at[n, x]
                )
            )
            stores[-1].start()
    for store in stores:
        store.wait()


def solution(mesh):
    counts = (mesh.shape["we"], mesh.shape["sn"])
    f32 = jnp.float32

    def shards(velocity, stress, memory, code, scale, table, cells, amps):
        velocity, stress, memory = (
            jnp.transpose(a, (0, 2, 1, 3)) for a in (velocity, stress, memory)
        )
        code = jnp.transpose(code, (1, 0, 2))
        scale = jnp.transpose(scale, (1, 0, 2))
        hbm = pl.BlockSpec(memory_space=pltpu.HBM)
        operands = [
            pltpu.with_memory_space_constraint(a, pltpu.HBM)
            for a in (velocity, stress, memory, code, scale, table, cells, amps)
        ]
        vmem = pl.BlockSpec(memory_space=pltpu.VMEM)
        fields = pl.pallas_call(
            functools.partial(kernel, counts),
            out_shape=(
                pltpu.VMEM((3, LAYERS, ROWS, 128), f32),
                pltpu.VMEM((6, 4, ROWS, 128), f32),
                pltpu.VMEM((6, 4, ROWS, 128), f32),
            ),
            in_specs=[hbm] * 8,
            out_specs=(vmem,) * 3,
            scratch_shapes=[
                pltpu.VMEM((LAYERS, ROWS, 128), jnp.int32),
                pltpu.VMEM((3, LAYERS, ROWS, 128), f32),
                pltpu.VMEM((3, 4, ROWS, 128), f32),
                pltpu.VMEM((2, 3, LAYERS, ROWS, 128), f32),
                pltpu.VMEM((2, 3, LAYERS, ROWS, 128), f32),
                pltpu.VMEM((LAYERS, ROWS, 128), f32),
                pltpu.VMEM((7, 4, ROWS, 128), f32),
                pltpu.VMEM((STEPS, 4, ROWS, 128), f32),
                pltpu.SMEM(scale.shape, f32),
                pltpu.SMEM(table.shape, f32),
                pltpu.SMEM(cells.shape, jnp.int32),
                pltpu.SMEM(amps.shape, f32),
                pltpu.SemaphoreType.DMA((4, 4)),
                pltpu.SemaphoreType.DMA((4,)),
                pltpu.SemaphoreType.DMA((4, 2)),
                pltpu.SemaphoreType.DMA((4, 2)),
                pltpu.SemaphoreType.DMA((2, 8, 3)),
                pltpu.SemaphoreType.DMA((2, 8, 3)),
            ],
            compiler_params=pltpu.CompilerParams(
                collective_id=0, has_side_effects=True, vmem_limit_bytes=16 * 1024 * 1024
            ),
        )(*operands)
        outs = pl.pallas_call(
            write_out,
            out_shape=tuple(
                jax.ShapeDtypeStruct(a.shape, f32) for a in (velocity, stress, memory)
            ),
            in_specs=[vmem] * 3,
            out_specs=(hbm,) * 3,
            scratch_shapes=[pltpu.SemaphoreType.DMA((3, 4))],
            compiler_params=pltpu.CompilerParams(vmem_limit_bytes=4 * 1024 * 1024),
        )(*(pltpu.with_memory_space_constraint(a, pltpu.VMEM) for a in fields))
        return tuple(jnp.transpose(a, (0, 2, 1, 3)) for a in outs)

    in_specs = (
        P(None, "we", "sn", None),
        P(None, "we", "sn", None),
        P(None, "we", "sn", None),
        P("we", "sn", None),
        P("we", "sn", None),
        P(),
        P("we", "sn", None),
        P("we", "sn", None, None),
    )
    out_specs = (P(None, "we", "sn", None),) * 3
    return jax.shard_map(shards, mesh=mesh, in_specs=in_specs, out_specs=out_specs, check_vma=False)
```

```python
import functools

import jax
import jax.numpy as jnp
from jax import lax
from jax.experimental import pallas as pl
from jax.experimental.pallas import tpu as pltpu
from jax.sharding import PartitionSpec as P

STEPS = 4
BLK = 4
BLKZ = 32
MESH = pl.DeviceIdType.MESH

inner_coef = 9.0 / 8.0
outer_coef = 1.0 / 24.0
time_step = 0.08
friction = 0.4
log2_e = 1.4426950408889634
ln_2 = 0.6931471805599453

LAYERS = 8
ROWS = 16

TO_HIGH = ((4, 0), (5, 1), (5, 1))
TO_LOW = ((0, 4), (1, 5), (1, 5))


def forward(layers, i):
    return combine(layers, (i + 1, i, i + 2, i - 1))


def backward(layers, i):
    return combine(layers, (i, i - 1, i + 1, i - 2))


def combine(layers, at):
    terms = []
    for index, coef in zip(at, (inner_coef, -inner_coef, -outer_coef, outer_coef)):
        if 0 <= index < len(layers):
            terms.append((coef, layers[index]))
    total = None
    for coef, layer in terms:
        total = coef * layer if total is None else total + coef * layer
    return total


def moved(field, offset, axis):
    size = field.shape[axis]
    return pltpu.roll(field, (-offset) % size, axis)


def forward_rows(field):
    return inner_coef * (moved(field, 1, 1) - field) - outer_coef * (
        moved(field, 2, 1) - moved(field, -1, 1)
    )


def backward_rows(field):
    return inner_coef * (field - moved(field, -1, 1)) - outer_coef * (
        moved(field, 1, 1) - moved(field, -2, 1)
    )


def kernel(
    counts,
    vel_in,
    str_in,
    mem_in,
    code_in,
    scale_in,
    table_in,
    cells_in,
    amps_in,
    V,
    S,
    M,
    CODE,
    G,
    GY,
    RA,
    RB,
    DB,
    PROP,
    SRC,
    scale,
    table,
    cells,
    amps,
    load_sem,
    small_sem,
    first_send,
    first_recv,
    send_sem,
    recv_sem,
):
    n_we, n_sn = counts
    we = lax.axis_index("we")
    sn = lax.axis_index("sn")
    side = {
        0: we,
        1: jnp.minimum(we + 1, n_we - 1),
        -1: jnp.maximum(we - 1, 0),
    }
    along_sn = {
        0: sn,
        1: jnp.minimum(sn + 1, n_sn - 1),
        -1: jnp.maximum(sn - 1, 0),
    }
    has_x = {1: we < n_we - 1, -1: we > 0}
    has_y = {1: sn < n_sn - 1, -1: sn > 0}

    def there(dx, dy):
        if dx and dy:
            return has_x[dx] & has_y[dy]
        return has_x[dx] if dx else has_y[dy]

    around = [(dx, dy) for dx in (1, -1) for dy in (1, -1)]
    around += [(0, 1), (0, -1), (1, 0), (-1, 0)]

    RA[0] = jnp.zeros((3, LAYERS, ROWS, 128), jnp.float32)
    RB[0] = jnp.zeros((3, LAYERS, ROWS, 128), jnp.float32)

    barrier = pltpu.get_barrier_semaphore()
    for dx, dy in around:

        @pl.when(there(dx, dy))
        def _():
            pl.semaphore_signal(
                barrier, inc=1, device_id=(side[dx], along_sn[dy]), device_id_type=MESH
            )

    loads = []
    for n, (src, dst, first) in enumerate(((str_in, S, 0), (code_in, CODE, 2), (vel_in, V, 2), (mem_in, M, 0))):
        for x in range(4):
            if src is code_in:
                pair = src.at[:, x, :], dst.at[first + x, 2:14, :]
            else:
                pair = src.at[:, :, x, :], dst.at[:, first + x, 2:14, :]
            loads.append(pltpu.make_async_copy(*pair, load_sem.at[n, x]))
            loads[-1].start()
    small = [
        pltpu.make_async_copy(src, dst, small_sem.at[n])
        for n, (src, dst) in enumerate(
            ((scale_in, scale), (table_in, table), (cells_in, cells), (amps_in, amps))
        )
    ]
    for load in small:
        load.start()

    edge_rows = jnp.zeros((6, 4, 2, 128), jnp.float32)
    S[:, :, 0:2, :] = edge_rows
    S[:, :, 14:16, :] = edge_rows
    G[0, 7] = jnp.zeros((ROWS, 128), jnp.float32)
    G[1, 0] = jnp.zeros((ROWS, 128), jnp.float32)
    G[2, 0] = jnp.zeros((ROWS, 128), jnp.float32)
    RA[1] = jnp.zeros((3, LAYERS, ROWS, 128), jnp.float32)
    RB[1] = jnp.zeros((3, LAYERS, ROWS, 128), jnp.float32)

    block = (4, ROWS, 128)
    lane = lax.broadcasted_iota(jnp.int32, (1, 1, 128), 2)
    row = lax.broadcasted_iota(jnp.int32, (1, ROWS, 128), 1)

    def lane_coef(coef, offset):
        inside = (lane + offset >= 0) & (lane + offset < 128)
        return jnp.where(inside, coef, 0.0)

    def forward_lanes(field):
        return (
            lane_coef(inner_coef, 1) * moved(field, 1, 2)
            - inner_coef * field
            - lane_coef(outer_coef, 2) * moved(field, 2, 2)
            + lane_coef(outer_coef, -1) * moved(field, -1, 2)
        )

    def backward_lanes(field):
        return (
            inner_coef * field
            - lane_coef(inner_coef, -1) * moved(field, -1, 2)
            - lane_coef(outer_coef, 1) * moved(field, 1, 2)
            + lane_coef(outer_coef, -2) * moved(field, -2, 2)
        )

    along = (forward, backward, backward)
    along_field = (0, 2, 1)

    def rim_forces():
        sxy, syz, syy = S[2], S[3], S[4]
        GY[0] = backward_rows(sxy)
        GY[1] = forward_rows(syy)
        GY[2] = backward_rows(syz)
        for c in range(3):
            layers = [S[along_field[c], x] for x in range(4)]
            for i in (-2, -1, 4, 5):
                part = along[c](layers, i)
                if part is not None:
                    G[c, i + 2] = part

    def own_forces():
        depth = (backward_lanes(S[1]), backward_lanes(S[3]), forward_lanes(S[5]))
        for c in range(3):
            layers = [S[along_field[c], x] for x in range(4)]
            rest = GY[c] + depth[c]
            for i in range(4):
                G[c, i + 2] = along[c](layers, i) + rest[i]

    everything = slice(None)

    def first_copies(dx, dy):
        if dx and dy:
            return []
        k = {(1, 0): 0, (-1, 0): 1, (0, 1): 2, (0, -1): 3}[dx, dy]
        here, into = {
            (1, 0): ((pl.ds(4, 2), pl.ds(2, 12)), (pl.ds(0, 2), pl.ds(2, 12))),
            (-1, 0): ((pl.ds(2, 2), pl.ds(2, 12)), (pl.ds(6, 2), pl.ds(2, 12))),
            (0, 1): ((pl.ds(2, 4), pl.ds(12, 2)), (pl.ds(2, 4), pl.ds(0, 2))),
            (0, -1): ((pl.ds(2, 4), pl.ds(2, 2)), (pl.ds(2, 4), pl.ds(14, 2))),
        }[dx, dy]
        pairs = [
            (V.at[(everything,) + here], V.at[(everything,) + into]),
            (CODE.at[here], CODE.at[into]),
        ]
        return [
            pltpu.make_async_remote_copy(
                src_ref=src,
                dst_ref=dst,
                send_sem=first_send.at[k, n],
                recv_sem=first_recv.at[k, n],
                device_id=(side[dx], along_sn[dy]),
                device_id_type=MESH,
            )
            for n, (src, dst) in enumerate(pairs)
        ]

    def step_copies(t, dx, dy):
        slot = lax.rem(t, 2)
        plan = []
        if dx and dy:
            from_l, to_l = (6, 2) if dx == 1 else (0, 4)
            from_r, to_r = (12, 0) if dy == 1 else (2, 14)
            plan.append((G, everything, from_l, 2, from_r, 2, RA, to_l, to_r))
            from_l, to_l = (2, 0) if dx == 1 else (0, 6)
            from_r, to_r = (14, 2) if dy == 1 else (0, 12)
            plan.append((GY, everything, from_l, 2, from_r, 2, RB, to_l, to_r))
        elif dy:
            from_r, to_r = (12, 0) if dy == 1 else (0, 12)
            plan.append((G, everything, 2, 4, from_r, 4, RB, 2, to_r))
        else:
            for c in range(3):
                from_l, to_l = (TO_HIGH if dx == 1 else TO_LOW)[c]
                plan.append((G, c, from_l, 3, 2, 12, RA, to_l, 2))
        k = around.index((dx, dy))
        return [
            pltpu.make_async_remote_copy(
                src_ref=field.at[c, pl.ds(from_l, n_l), pl.ds(from_r, n_r), :],
                dst_ref=ref.at[slot, c, pl.ds(to_l, n_l), pl.ds(to_r, n_r), :],
                send_sem=send_sem.at[slot, k, n],
                recv_sem=recv_sem.at[slot, k, n],
                device_id=(side[dx], along_sn[dy]),
                device_id_type=MESH,
            )
            for n, (field, c, from_l, n_l, from_r, n_r, ref, to_l, to_r) in enumerate(plan)
        ]

    diagonal, sides = around[:4], around[4:]

    def start_all(copies_of, which):
        for dx, dy in which:

            @pl.when(there(dx, dy))
            def _():
                for copy in copies_of(dx, dy):
                    copy.start()

    def wait_all(copies_of, which, received):
        for dx, dy in which:

            @pl.when(there(-dx, -dy) if received else there(dx, dy))
            def _():
                for copy in copies_of(dx, dy):
                    if received:
                        copy.wait_recv()
                    else:
                        copy.wait_send()

    for load in loads[:4]:
        load.wait()
    rim_forces()
    own_forces()
    for load in loads[4:]:
        load.wait()

    n_x = 1 + has_x[1].astype(jnp.int32) + has_x[-1].astype(jnp.int32)
    n_y = 1 + has_y[1].astype(jnp.int32) + has_y[-1].astype(jnp.int32)
    pl.semaphore_wait(barrier, n_x * n_y - 1)
    start_all(functools.partial(step_copies, 0), diagonal)
    start_all(first_copies, sides)
    start_all(functools.partial(step_copies, 0), sides)
    for load in small:
        load.wait()

    def look_up(code, r):
        values = [table[r, k] for k in range(16)]
        for bit in range(4):
            chosen = (code & (1 << bit)) != 0
            values = [
                jnp.where(chosen, values[2 * k + 1], values[2 * k])
                for k in range(len(values) // 2)
            ]
        return values[0]

    moduli = jnp.zeros((1, ROWS, 128), jnp.float32)
    for j in range(3):
        for k in range(128 // BLKZ):
            here = (
                (row >= 2 + BLK * j)
                & (row < 2 + BLK * (j + 1))
                & (lane >= BLKZ * k)
                & (lane < BLKZ * (k + 1))
            )
            moduli = jnp.where(here, scale[j, 0, k], moduli)
    code = CODE[2:6, 2:14]

    def keep(n, value):
        PROP[n, :, 2:14] = value

    own_moduli = moduli[:, 2:14]
    keep(0, look_up(code, 1) * own_moduli)
    keep(1, look_up(code, 2) * own_moduli)
    decay = look_up(code, 3)
    gain = (1.0 - decay) * look_up(code, 4)
    keep(2, decay)
    keep(3, gain)
    keep(4, time_step * (1.0 - 0.5 * gain))
    keep(5, (0.5 * time_step) * (1.0 + decay))
    keep(6, look_up(code, 5))

    cell = (
        (
            lax.broadcasted_iota(jnp.int32, block, 0) * 12
            + lax.broadcasted_iota(jnp.int32, block, 1)
            - 2
        )
        * 128
        + lax.broadcasted_iota(jnp.int32, block, 2)
    )
    for n in range(STEPS):
        added = jnp.zeros(block, jnp.float32)
        for k in range(4):
            added = added + jnp.where(
                cell == cells[0, 0, k], time_step * amps[0, 0, k, n], 0.0
            )
        SRC[n] = added

    wait_all(first_copies, sides, True)
    wait_all(first_copies, sides, False)

    layer = lax.broadcasted_iota(jnp.int32, (LAYERS, ROWS, 128), 0)
    rows = lax.broadcasted_iota(jnp.int32, (LAYERS, ROWS, 128), 1)
    inside = (
        (layer >= jnp.where(we == 0, 2, 0))
        & (layer < jnp.where(we == n_we - 1, 6, 8))
        & (rows >= jnp.where(sn == 0, 2, 0))
        & (rows < jnp.where(sn == n_sn - 1, 14, 16))
    )
    DB[...] = jnp.where(inside, time_step * look_up(CODE[...], 0), 0.0)
    for c in range(3):
        V[c] = jnp.where(inside, V[c], 0.0)

    def step(t, carry):
        copies = functools.partial(step_copies, t)
        slot = lax.rem(t, 2)

        def advance(c, layers, rows):
            at = (layers, rows)
            arrived = RA[(slot, c) + at] + RB[(slot, c) + at]
            V[(c,) + at] = V[(c,) + at] + DB[at] * (G[(c,) + at] + arrived)

        wait_all(copies, sides, True)
        for c in range(3):
            advance(c, slice(2, 6), slice(2, 14))
        depth_of = (
            forward_lanes(V[0, 2:6]),
            forward_lanes(V[1, 2:6]),
            backward_lanes(V[2, 2:6]),
        )
        wait_all(copies, diagonal, True)
        for c in range(3):
            advance(c, slice(2, 6), slice(0, 2))
            advance(c, slice(2, 6), slice(14, 16))
            advance(c, slice(0, 2), slice(0, 16))
            advance(c, slice(6, 8), slice(0, 16))

        def forward_x(c):
            return inner_coef * (V[c, 3:7] - V[c, 2:6]) - outer_coef * (V[c, 4:8] - V[c, 1:5])

        def backward_x(c):
            return inner_coef * (V[c, 2:6] - V[c, 1:5]) - outer_coef * (V[c, 3:7] - V[c, 0:4])

        ve, vn, vd = (V[c, 2:6] for c in range(3))
        exx = backward_x(0)
        eyy = backward_rows(vn)
        ezz = depth_of[2]
        exz = depth_of[0] + forward_x(2)
        exy = forward_rows(ve) + forward_x(1)
        eyz = depth_of[1] + forward_rows(vd)
        lame, shear = PROP[0], PROP[1]
        volume = lame * (exx + eyy + ezz)
        twice = shear + shear
        rates = (
            volume + twice * exx,
            shear * exz,
            shear * exy,
            shear * eyz,
            volume + twice * eyy,
            volume + twice * ezz,
        )
        trial = []
        for c in range(6):
            memory = M[c]
            M[c] = PROP[2] * memory + PROP[3] * rates[c]
            trial.append(S[c] + PROP[4] * rates[c] - PROP[5] * memory)
        added = SRC[t]
        for c in (0, 4, 5):
            trial[c] = trial[c] + added
        mean = (trial[0] + trial[4] + trial[5]) * (1.0 / 3.0)
        for c in (0, 4, 5):
            trial[c] = trial[c] - mean
        normal = trial[0] * trial[0] + trial[4] * trial[4] + trial[5] * trial[5]
        second = 0.5 * normal + (
            trial[1] * trial[1] + trial[2] * trial[2] + trial[3] * trial[3]
        )
        soft = jnp.maximum(-mean, 0.0) + ln_2 * jnp.log2(1.0 + jnp.exp2(-log2_e * jnp.abs(mean)))
        level = PROP[6] + friction * soft
        scaled = second / (level * level)
        factor = jnp.exp2(-0.25 * jnp.log2(1.0 + scaled * scaled))
        own = (row >= 2) & (row < 14)
        for c in range(6):
            new = factor * trial[c]
            if c in (0, 4, 5):
                new = mean + new
            S[c] = jnp.where(own, new, 0.0)

        wait_all(copies, around, False)

        @pl.when(t < STEPS - 1)
        def _():
            later = functools.partial(step_copies, t + 1)
            rim_forces()
            start_all(later, diagonal)
            own_forces()
            start_all(later, sides)

        return carry

    lax.fori_loop(0, STEPS, step, 0)


def write_out(V, S, M, vel_out, str_out, mem_out, sem):
    stores = []
    for n, (src, first, dst) in enumerate(((V, 2, vel_out), (S, 0, str_out), (M, 0, mem_out))):
        for x in range(4):
            stores.append(
                pltpu.make_async_copy(
                    src.at[:, first + x, pl.ds(2, 12), :], dst.at[:, :, x, :], sem.at[n, x]
                )
            )
            stores[-1].start()
    for store in stores:
        store.wait()


def solution(mesh):
    counts = (mesh.shape["we"], mesh.shape["sn"])
    f32 = jnp.float32

    def shards(velocity, stress, memory, code, scale, table, cells, amps):
        velocity, stress, memory = (
            jnp.transpose(a, (0, 2, 1, 3)) for a in (velocity, stress, memory)
        )
        code = jnp.transpose(code, (1, 0, 2))
        scale = jnp.transpose(scale, (1, 0, 2))
        hbm = pl.BlockSpec(memory_space=pltpu.HBM)
        operands = [
            pltpu.with_memory_space_constraint(a, pltpu.HBM)
            for a in (velocity, stress, memory, code, scale, table, cells, amps)
        ]
        vmem = pl.BlockSpec(memory_space=pltpu.VMEM)
        fields = pl.pallas_call(
            functools.partial(kernel, counts),
            out_shape=(
                pltpu.VMEM((3, LAYERS, ROWS, 128), f32),
                pltpu.VMEM((6, 4, ROWS, 128), f32),
                pltpu.VMEM((6, 4, ROWS, 128), f32),
            ),
            in_specs=[hbm] * 8,
            out_specs=(vmem,) * 3,
            scratch_shapes=[
                pltpu.VMEM((LAYERS, ROWS, 128), jnp.int32),
                pltpu.VMEM((3, LAYERS, ROWS, 128), f32),
                pltpu.VMEM((3, 4, ROWS, 128), f32),
                pltpu.VMEM((2, 3, LAYERS, ROWS, 128), f32),
                pltpu.VMEM((2, 3, LAYERS, ROWS, 128), f32),
                pltpu.VMEM((LAYERS, ROWS, 128), f32),
                pltpu.VMEM((7, 4, ROWS, 128), f32),
                pltpu.VMEM((STEPS, 4, ROWS, 128), f32),
                pltpu.SMEM(scale.shape, f32),
                pltpu.SMEM(table.shape, f32),
                pltpu.SMEM(cells.shape, jnp.int32),
                pltpu.SMEM(amps.shape, f32),
                pltpu.SemaphoreType.DMA((4, 4)),
                pltpu.SemaphoreType.DMA((4,)),
                pltpu.SemaphoreType.DMA((4, 2)),
                pltpu.SemaphoreType.DMA((4, 2)),
                pltpu.SemaphoreType.DMA((2, 8, 3)),
                pltpu.SemaphoreType.DMA((2, 8, 3)),
            ],
            compiler_params=pltpu.CompilerParams(
                collective_id=0, has_side_effects=True, vmem_limit_bytes=16 * 1024 * 1024
            ),
        )(*operands)
        outs = pl.pallas_call(
            write_out,
            out_shape=tuple(
                jax.ShapeDtypeStruct(a.shape, f32) for a in (velocity, stress, memory)
            ),
            in_specs=[vmem] * 3,
            out_specs=(hbm,) * 3,
            scratch_shapes=[pltpu.SemaphoreType.DMA((3, 4))],
            compiler_params=pltpu.CompilerParams(vmem_limit_bytes=4 * 1024 * 1024),
        )(*(pltpu.with_memory_space_constraint(a, pltpu.VMEM) for a in fields))
        return tuple(jnp.transpose(a, (0, 2, 1, 3)) for a in outs)

    in_specs = (
        P(None, "we", "sn", None),
        P(None, "we", "sn", None),
        P(None, "we", "sn", None),
        P("we", "sn", None),
        P("we", "sn", None),
        P(),
        P("we", "sn", None),
        P("we", "sn", None, None),
    )
    out_specs = (P(None, "we", "sn", None),) * 3
    return jax.shard_map(shards, mesh=mesh, in_specs=in_specs, out_specs=out_specs, check_vma=False)
```
